32 devices in a mesh: groups: 2 (over y), store: 16 (over z, x, core).
Axes of the slice: x: 2, y: 2, z: 4, core: 2. Of those that a mesh axis runs over, the one named last changes fastest.
Arguments:
- queries: bfloat16 [2, 32, 8192], P(None, ('groups', 'store')), parts along dimension 1, may hold values from -6 to 206
- new_keys: bfloat16 [2, 32, 1024], P(None, ('groups', 'store')), parts along dimension 1, may hold values from -6 to 12.5
- incoming_values: bfloat16 [2, 32, 1024], P(None, ('groups', 'store')), parts along dimension 1, may hold values from -6 to 6
- key_left: bfloat16 [32, 4096, 160], P(('groups', 'store')), parts along dimension 0, may hold values from -12 to 12
- right_key_factor: bfloat16 [32, 160, 1024], P(('groups', 'store')), parts along dimension 0, may hold values from -0.5 to 0.5
- value_tile_store: bfloat16 [131072, 1024], P(('groups', 'store')), parts along dimension 0, may hold values from -6 to 6
- slot_map: int32 [32, 8, 512], P(('groups', 'store')), parts along dimension 0, may hold values from 0 to 65535, as said below
- chosen: int32 [2, 32, 8, 64], P(None, ('groups', 'store')), parts along dimension 1, may hold values from 0 to 511, as said below
- lengths: int32 [32], P(('groups', 'store')), parts along dimension 0, may hold values from 1024 to 4096
Outputs:
- attended: bfloat16 [2, 32, 8192], P(None, ('groups', 'store')), parts along dimension 1
The draws below stay inside these ranges and needn't reach their ends.
There are 2 independent parts, one for each index of `groups`. The reference program is written for one: setup_inputs(seed, part) draws one part's arguments, and reference() takes and returns one part's arrays. A program takes and returns all parts, laid end to end along the dimension named above; each array names one. Nothing has to cross between parts.
Inputs may be any that keep to these rules, and one draw needn't show every extreme that they name: `slot_map`: the entries are distinct; pool rows r * 4096 to (r+1) * 4096 - 1 stand on index r of store. `chosen`: the 64 blocks of one step, request and key head are distinct; at most 8 of them have their slot_map row on one index of store, and in every step some index of store holds exactly 8 of them for every request and key head.
All inputs are finite; a program needn't handle non-finite values.
Results may differ from the reference program's by a relative error of at most 0.005.
The reference program's roundings to bfloat16 on the way count: a program that leaves them out, or rounds other values in their place, can miss the bound.
Values may be sent and summed in bfloat16 or wider, within the bound.
No kernel may reach another device: no remote copies, remote signals or barrier semaphores. Data moves between devices by JAX's collectives and lax.ppermute only.
A program may use at most 64 MiB of HBM per device.

```python
import jax
import jax.numpy as jnp
from jax import lax

QUERY_HEADS = 64
KEY_VALUE_HEADS = 8
HEAD_SIZE = 128
FACTOR_RANK = 160
BLOCK_TOKENS = 8
SELECTED_BLOCKS = 64
DECODE_STEPS = 2
CTX = 4096
TOTAL_REQUESTS = 16
CACHE_BLOCKS = 512
PER_HOLDER = 8
DEVICE_TILES = 4096
POOL = 65536
N_STORE = 16


def layout(key):
    child_seed = jax.random.fold_in(key, 11)
    child_seeds = jax.random.split(child_seed, TOTAL_REQUESTS * KEY_VALUE_HEADS)
    tile_ordering = jax.vmap(lambda single: jax.random.permutation(single, CACHE_BLOCKS))(child_seeds)
    return tile_ordering.reshape(TOTAL_REQUESTS, KEY_VALUE_HEADS, CACHE_BLOCKS).astype(jnp.int32)


def draw_slot_map(key, part):
    tile_ordering = layout(key)
    device_share = CACHE_BLOCKS // N_STORE
    tile_keeper = tile_ordering // device_share
    inner_offset = tile_ordering % device_share
    row_ids = jnp.arange(TOTAL_REQUESTS, dtype=jnp.int32)[:, None, None]
    head_numbers = jnp.arange(KEY_VALUE_HEADS, dtype=jnp.int32)[None, :, None]
    canonical = (row_ids * KEY_VALUE_HEADS + head_numbers) * device_share + inner_offset
    holder_seeds = jax.random.split(jax.random.fold_in(key, 13), N_STORE)
    holder_orders = jax.vmap(lambda single: jax.random.permutation(single, DEVICE_TILES))(holder_seeds).astype(jnp.int32)
    placed = holder_orders[tile_keeper, canonical]
    return (tile_keeper * DEVICE_TILES + placed).astype(jnp.int32)


def draw_chosen(key, part):
    tile_ordering = layout(key)
    device_share = CACHE_BLOCKS // N_STORE
    tile_keeper = tile_ordering // device_share
    inner_offset = tile_ordering % device_share
    block_numbers = jnp.arange(CACHE_BLOCKS, dtype=jnp.int32)
    picks = []
    for step_index in range(DECODE_STEPS):
        step_key = jax.random.fold_in(key, 100 + step_index)
        heat_key, hot_key, noise_seed, window_key = jax.random.split(step_key, 4)
        window_start = jax.random.randint(window_key, (TOTAL_REQUESTS, KEY_VALUE_HEADS, N_STORE), 0, device_share).astype(jnp.int32)
        start_here = jnp.take_along_axis(window_start, tile_keeper, axis=2)
        eligible = (inner_offset - start_here + device_share) % device_share < PER_HOLDER
        heat_level = jax.random.randint(heat_key, (N_STORE,), 0, 4)
        hottest = jax.random.randint(hot_key, (), 0, N_STORE)
        heat_level = jnp.where(jnp.arange(N_STORE) == hottest, 16, heat_level)
        random_noise = jax.random.randint(noise_seed, (TOTAL_REQUESTS, KEY_VALUE_HEADS, CACHE_BLOCKS), 0, 4096)
        scores = jnp.where(eligible, (heat_level[tile_keeper] + 1) * (4096 * CACHE_BLOCKS) + random_noise * CACHE_BLOCKS + block_numbers, block_numbers)
        top_idx = lax.top_k(scores.astype(jnp.int32), SELECTED_BLOCKS)[1]
        picks.append(top_idx.astype(jnp.int32))
    return jnp.stack(picks)


def draw_queries(key, part):
    gaussian_seed = jax.random.fold_in(jax.random.fold_in(key, 21), 0)
    sampled_blocks = jnp.clip(jax.random.normal(gaussian_seed, (DECODE_STEPS, TOTAL_REQUESTS, QUERY_HEADS, HEAD_SIZE), jnp.float32), -6.0, 6.0)
    return sampled_blocks.reshape(DECODE_STEPS, TOTAL_REQUESTS, QUERY_HEADS * HEAD_SIZE).astype(jnp.bfloat16)


def draw_new_keys(key, part):
    gaussian_seed = jax.random.fold_in(jax.random.fold_in(key, 31), 0)
    sampled_blocks = jnp.clip(jax.random.normal(gaussian_seed, (DECODE_STEPS, TOTAL_REQUESTS, KEY_VALUE_HEADS, HEAD_SIZE), jnp.float32), -6.0, 6.0)
    sampled_blocks = jnp.clip(sampled_blocks, -6.0, 12.5)
    return sampled_blocks.reshape(DECODE_STEPS, TOTAL_REQUESTS, KEY_VALUE_HEADS * HEAD_SIZE).astype(jnp.bfloat16)


def touch_ends(entries, rng, low, largest):
    spot = [jax.random.randint(jax.random.fold_in(rng, axis), (), 0, length) for axis, length in enumerate(entries.shape)]
    longest = entries.shape.index(max(entries.shape))
    beside = spot[:longest] + [(spot[longest] + 1) % entries.shape[longest]] + spot[longest + 1:]
    return entries.at[tuple(spot)].set(low).at[tuple(beside)].set(largest)


def block_scale(key, dims, cuts, low, largest):
    def one(axis_at, shards_of):
        heights = jax.random.uniform(jax.random.fold_in(jax.random.fold_in(key, 6), axis_at), (shards_of,), jnp.float32, low / len(cuts), largest / len(cuts))
        return jnp.repeat(jnp.exp(heights), dims[axis_at] // shards_of).reshape((-1,) + (1,) * (len(dims) - axis_at - 1))

    factor_of = one(*cuts[0])
    for cut in cuts[1:]:
        factor_of = factor_of * one(*cut)
    return factor_of


def centred(stream_key, dims, deviation, bound, cuts=(), kind=jnp.bfloat16):
    result = jax.random.normal(stream_key, dims, jnp.float32) * deviation
    if len(cuts) > 0:
        result = block_scale(stream_key, dims, cuts, -0.22, 0.18) * result
    return jnp.clip(result, min=-bound, max=bound).astype(kind)


def setup_inputs(seed: int = 0, part: int = 0) -> dict:
    keys = jax.random.split(jax.random.key(seed), 10)
    own_keys = jax.random.split(jax.random.fold_in(keys[9], part), 10)
    queries = draw_queries(jax.random.fold_in(jax.random.fold_in(keys[9], part), 71), part)
    new_keys = draw_new_keys(jax.random.fold_in(jax.random.fold_in(keys[9], part), 71), part)
    incoming_values = centred(own_keys[2], (DECODE_STEPS, TOTAL_REQUESTS, KEY_VALUE_HEADS * HEAD_SIZE), 1.0, 6.0, ((1, 16),))
    key_left = centred(own_keys[3], (TOTAL_REQUESTS, CTX, FACTOR_RANK), 2.0, 12.0, ((0, 16),))
    right_key_factor = centred(own_keys[4], (TOTAL_REQUESTS, FACTOR_RANK, KEY_VALUE_HEADS * HEAD_SIZE), FACTOR_RANK ** -0.5, 0.5, ((0, 16),))
    value_tile_store = centred(own_keys[5], (POOL, BLOCK_TOKENS * HEAD_SIZE), 1.0, 6.0, ((0, 16),))
    slot_map = draw_slot_map(jax.random.fold_in(jax.random.fold_in(keys[9], part), 71), part)
    chosen = draw_chosen(jax.random.fold_in(jax.random.fold_in(keys[9], part), 71), part)
    lengths = touch_ends(jax.random.randint(own_keys[8], (TOTAL_REQUESTS,), CTX // 4, CTX + 1), jax.random.fold_in(own_keys[8], 1), CTX // 4, CTX).astype(jnp.int32)
    return {"queries": queries, "new_keys": new_keys, "incoming_values": incoming_values, "key_left": key_left, "right_key_factor": right_key_factor, "value_tile_store": value_tile_store, "slot_map": slot_map, "chosen": chosen, "lengths": lengths}


ROPE_BASE = 500000.0


def apply_rotary(tensor, token_positions):
    half_dim = tensor.shape[-1] // 2
    inverse = ROPE_BASE ** (-(jnp.arange(half_dim, dtype=jnp.float32) * 2.0 / tensor.shape[-1]))
    angles = jnp.asarray(token_positions).astype(jnp.float32)[..., None] * inverse
    cosine = jnp.cos(angles)
    sine_vals = jnp.sin(angles)
    first_half = tensor[..., :half_dim]
    second_half = tensor[..., half_dim:]
    return jnp.concatenate([first_half * cosine - second_half * sine_vals, second_half * cosine + first_half * sine_vals], -1)


def reference(queries, new_keys, incoming_values, key_left, right_key_factor, value_tile_store, slot_map, chosen, lengths):
    query_group_size = QUERY_HEADS // KEY_VALUE_HEADS
    score_scale = HEAD_SIZE ** -0.5

    def row_fn(per_row):
        query_full, incoming_keys_full, incoming_values_full, left_rows, right_factor_rows, slot_row, chosen_row, length = per_row
        right_factor_heads = right_factor_rows.reshape(FACTOR_RANK, KEY_VALUE_HEADS, HEAD_SIZE).astype(jnp.float32)
        results = []
        for step_index in range(DECODE_STEPS):
            block_numbers = chosen_row[step_index]
            token_positions = (block_numbers[:, :, None] * BLOCK_TOKENS + jnp.arange(BLOCK_TOKENS, dtype=jnp.int32)).reshape(KEY_VALUE_HEADS, SELECTED_BLOCKS * BLOCK_TOKENS)
            picked = left_rows[token_positions].astype(jnp.float32)
            raw_keys = jnp.einsum('htr,rhd->htd', picked, right_factor_heads)
            cache_keys = apply_rotary(raw_keys, token_positions).astype(jnp.bfloat16)
            rotated_query = apply_rotary(query_full[step_index].reshape(QUERY_HEADS, HEAD_SIZE).astype(jnp.float32), length + step_index).astype(jnp.bfloat16)
            current_position = (length + jnp.arange(step_index + 1, dtype=jnp.int32))[:, None]
            current_keys = apply_rotary(incoming_keys_full[:step_index + 1].reshape(step_index + 1, KEY_VALUE_HEADS, HEAD_SIZE).astype(jnp.float32), current_position).astype(jnp.bfloat16)
            current_keys = jnp.transpose(current_keys, (1, 0, 2))
            current_values = jnp.transpose(incoming_values_full[:step_index + 1].reshape(step_index + 1, KEY_VALUE_HEADS, HEAD_SIZE), (1, 0, 2))
            slot_numbers = jnp.take_along_axis(slot_row, block_numbers, axis=1)
            tile_row_index = value_tile_store[slot_numbers].reshape(KEY_VALUE_HEADS, SELECTED_BLOCKS * BLOCK_TOKENS, HEAD_SIZE)
            grouped_queries = rotated_query.reshape(KEY_VALUE_HEADS, query_group_size, HEAD_SIZE).astype(jnp.float32)
            cache_scores = jnp.einsum('hgd,htd->hgt', grouped_queries, cache_keys.astype(jnp.float32)) * score_scale
            inside_len = token_positions < length
            cache_scores = jnp.where(inside_len[:, None, :], cache_scores, -jnp.inf)
            fresh_scores = jnp.einsum('hgd,hnd->hgn', grouped_queries, current_keys.astype(jnp.float32)) * score_scale
            highest = jnp.maximum(jnp.max(cache_scores, -1, keepdims=True), jnp.max(fresh_scores, -1, keepdims=True))
            cache_exp = jnp.exp(cache_scores - highest)
            fresh_exp = jnp.exp(fresh_scores - highest)
            denominator = jnp.sum(cache_exp, -1, keepdims=True) + jnp.sum(fresh_exp, -1, keepdims=True)
            cache_weight = (cache_exp / denominator).astype(jnp.bfloat16)
            fresh_weight = (fresh_exp / denominator).astype(jnp.bfloat16)
            attended = jnp.einsum('hgt,htd->hgd', cache_weight.astype(jnp.float32), tile_row_index.astype(jnp.float32))
            attended = attended + jnp.einsum('hgn,hnd->hgd', fresh_weight.astype(jnp.float32), current_values.astype(jnp.float32))
            results.append(attended.reshape(QUERY_HEADS * HEAD_SIZE).astype(jnp.bfloat16))
        return jnp.stack(results)

    per_row = (jnp.transpose(queries, (1, 0, 2)), jnp.transpose(new_keys, (1, 0, 2)), jnp.transpose(incoming_values, (1, 0, 2)), key_left, right_key_factor, slot_map, jnp.transpose(chosen, (1, 0, 2, 3)), lengths)
    output = lax.map(row_fn, per_row)
    return jnp.transpose(output, (1, 0, 2))
```

```python
import functools

import jax
import jax.numpy as jnp
import numpy as np
from jax import lax
from jax.experimental import pallas as pl
from jax.experimental.pallas import tpu as pltpu
from jax.sharding import PartitionSpec as P

HEAD_SIZE = 128
HALF = HEAD_SIZE // 2
BLOCK_TOKENS = 8
ROPE_BASE = 500000.0
NT = (((1,), (1,)), ((), ()))
NN = (((1,), (0,)), ((), ()))
F32 = jnp.float32
BF16 = jnp.bfloat16


def mm(a, b, dims=NN):
    return lax.dot_general(a, b, dims, preferred_element_type=F32)


def rope_tables(blocks):
    exponent = -(np.arange(HALF, dtype=np.float32) * np.float32(2.0) / np.float32(HEAD_SIZE))
    freq = (np.float32(ROPE_BASE) ** exponent).astype(np.float64)
    freq = np.concatenate([freq, freq])
    rows = np.arange(-(-(blocks + 2) // 8) * 8, dtype=np.float64)[:, None] * BLOCK_TOKENS
    offs = np.arange(BLOCK_TOKENS, dtype=np.float64)[:, None]
    base = np.stack([np.cos(rows * freq), np.sin(rows * freq)]).astype(np.float32)
    off = np.stack([np.cos(offs * freq), np.sin(offs * freq)]).astype(np.float32)
    return base, off


def owner_kernel(
    share, pool, len_ref, q_ref, nk_ref, iv_ref, kl_ref, rk_ref, sm_ref, ch_ref, tab_ref, off_ref,
    w_ref, fresh_ref,
    lf, sc, rp, qp, qr, fs_scr, fm_scr, fw_scr, m_scr, x_scr, cnt_scr, osc,
):
    tokens, rank = kl_ref.shape
    heads, blocks = sm_ref.shape
    combos = ch_ref.shape[0]
    steps = combos // heads
    n_sel = ch_ref.shape[1]
    rows = q_ref.shape[0]
    group = rows // combos
    slots = osc.shape[2]
    keepers = slots // share
    pairs = heads // 2
    parts = lf.shape[0]
    scale = HEAD_SIZE ** -0.5
    length = len_ref[0]
    lane = lax.broadcasted_iota(jnp.int32, (1, HEAD_SIZE), 1)
    low = lane < HALF

    def widen(i, _):
        s = pl.ds(pl.multiple_of(i * blocks, blocks), blocks)
        x = kl_ref[s, :].astype(F32)
        for d in range(parts):
            y = x[:, d * HEAD_SIZE:min(rank, (d + 1) * HEAD_SIZE)]
            if y.shape[1] < HEAD_SIZE:
                y = jnp.concatenate([y, jnp.zeros((blocks, HEAD_SIZE - y.shape[1]), F32)], axis=1)
            lf[d, s, :] = y
        return _

    lax.fori_loop(0, tokens // blocks, widen, 0)

    for p in range(pairs):
        r0 = rk_ref[:, (2 * p) * HEAD_SIZE:(2 * p + 1) * HEAD_SIZE].astype(F32)
        r1 = rk_ref[:, (2 * p + 1) * HEAD_SIZE:(2 * p + 2) * HEAD_SIZE].astype(F32)
        first = jnp.where(low, r0, pltpu.roll(r1, HALF, 1))
        second = jnp.where(low, pltpu.roll(r0, HALF, 1), r1)
        both = jnp.concatenate([first, second], axis=1)
        if rp.shape[1] > rank:
            both = jnp.concatenate([both, jnp.zeros((rp.shape[1] - rank, 2 * HEAD_SIZE), F32)], axis=0)
        rp[p] = both.astype(BF16)

    sign = jnp.where(low, -1.0, 1.0).astype(F32)

    def angle(position):
        b = position // BLOCK_TOKENS
        j = position - b * BLOCK_TOKENS
        cb = tab_ref[0, pl.ds(b, 1), :]
        sb = tab_ref[1, pl.ds(b, 1), :]
        cj = off_ref[0, pl.ds(j, 1), :]
        sj = off_ref[1, pl.ds(j, 1), :]
        return cb * cj - sb * sj, (sb * cj + cb * sj) * sign

    per_step = heads * group
    fresh_keys = []
    for s in range(steps):
        c, sn = angle(length + s)
        x = q_ref[s * per_step:(s + 1) * per_step, :].astype(F32)
        x = x * c + pltpu.roll(x, HALF, 1) * sn
        qr[s * per_step:(s + 1) * per_step, :] = x.astype(BF16).astype(F32)
        y = nk_ref[s * heads:(s + 1) * heads, :].astype(F32)
        fresh_keys.append(y * c + pltpu.roll(y, HALF, 1) * sn)
    fk = jnp.concatenate(fresh_keys, axis=0).astype(BF16)
    fs = mm(qr[...].astype(BF16), fk, NT) * scale
    ri = lax.broadcasted_iota(jnp.int32, fs.shape, 0)
    ci = lax.broadcasted_iota(jnp.int32, fs.shape, 1)
    keep = jnp.logical_and((ri // group) % heads == ci % heads, ci // heads <= ri // per_step)
    fs = jnp.where(keep, fs, -jnp.inf)
    fs_scr[...] = fs
    fm_scr[...] = jnp.max(fs, axis=1, keepdims=True)

    for p in range(pairs):
        pieces = []
        for s in range(steps):
            for hh in range(2):
                start = s * per_step + (2 * p + hh) * group
                x = qr[start:start + group, :]
                y = pltpu.roll(x, HALF, 1)
                if hh == 0:
                    pieces.append(jnp.concatenate([jnp.where(low, x, 0.0), jnp.where(low, y, 0.0)], axis=1))
                else:
                    pieces.append(jnp.concatenate([jnp.where(low, 0.0, y), jnp.where(low, 0.0, x)], axis=1))
        qp[p] = jnp.concatenate(pieces, axis=0).astype(BF16)

    def keys(j, _):
        lj = jnp.concatenate(
            [lf[d, pl.ds(j, blocks, stride=BLOCK_TOKENS), :] for d in range(parts)], axis=1
        ).astype(BF16)
        cj = off_ref[0, pl.ds(j, 1), :]
        sj = off_ref[1, pl.ds(j, 1), :]
        cb = tab_ref[0, :blocks, :]
        sb = tab_ref[1, :blocks, :]
        ct = cb * cj - sb * sj
        st = sb * cj + cb * sj
        for p in range(pairs):
            raw = mm(lj, rp[p])
            a = raw[:, :HEAD_SIZE]
            c = raw[:, HEAD_SIZE:]
            k = jnp.concatenate([a * ct - c * st, c * ct + a * st], axis=1).astype(BF16)
            out = mm(qp[p], k, NT)
            for s in range(steps):
                sc[j, s * per_step + 2 * p * group:s * per_step + 2 * (p + 1) * group, :] = (
                    out[s * 2 * group:(s + 1) * 2 * group, :]
                )
        return _

    lax.fori_loop(0, BLOCK_TOKENS, keys, 0)

    block_i = lax.broadcasted_iota(jnp.int32, (blocks, n_sel), 0)
    keeper_i = lax.broadcasted_iota(jnp.int32, (keepers, blocks), 0)
    ones = jnp.ones((8, n_sel), BF16)

    def choose(c, _):
        hot = jnp.where(block_i == ch_ref[pl.ds(c, 1), :], 1.0, 0.0).astype(BF16)
        m = mm(ones, hot, NT)
        m_scr[c] = m
        kb = sm_ref[pl.ds(c % heads, 1), :] // pool
        x = jnp.where(jnp.logical_and(keeper_i == kb, m[:1] > 0.5), 1.0, 0.0)
        x_scr[pl.ds(pl.multiple_of(c * keepers, keepers), keepers), :] = x.astype(BF16)
        return _

    lax.fori_loop(0, combos, choose, 0)
    tri = jnp.where(
        lax.broadcasted_iota(jnp.int32, (blocks, blocks), 0)
        < lax.broadcasted_iota(jnp.int32, (blocks, blocks), 1), 1.0, 0.0
    ).astype(BF16)
    cnt_scr[...] = mm(x_scr[...], tri)

    slot_i = lax.broadcasted_iota(jnp.int32, (slots, blocks), 0)
    pos0 = lax.broadcasted_iota(jnp.int32, (group, blocks), 1) * BLOCK_TOKENS
    sub = lax.broadcasted_iota(jnp.int32, (group, blocks), 0)
    planes = osc.shape[0]

    def weigh(c, _):
        here = pl.ds(pl.multiple_of(c * group, group), group)
        m = m_scr[c] > 0.5
        xs = []
        for j in range(BLOCK_TOKENS):
            ok = jnp.logical_and(m, pos0 + j < length)
            xs.append(jnp.where(ok, sc[j, here, :] * scale, -jnp.inf))
        top = functools.reduce(jnp.maximum, xs)
        top = jnp.maximum(jnp.max(top, axis=1, keepdims=True), fm_scr[here, :])
        es = [jnp.exp(x - top) for x in xs]
        fe = jnp.exp(fs_scr[here, :] - top)
        total = jnp.sum(functools.reduce(jnp.add, es), axis=1, keepdims=True)
        total = total + jnp.sum(fe, axis=1, keepdims=True)
        inv = 1.0 / total
        fw_scr[here, :] = fe * inv
        slot_row = sm_ref[pl.ds(c % heads, 1), :]
        kb = slot_row // pool
        inside = slot_row - kb * pool
        hi = inside // 256
        lo = inside - hi * 256
        extra = jnp.where(sub == 0, hi, jnp.where(sub == 1, lo, 0)).astype(F32)
        lhs = jnp.concatenate([e * inv for e in es] + [extra, jnp.zeros_like(extra)], axis=0).astype(BF16)
        mine = pl.ds(pl.multiple_of(c * keepers, keepers), keepers)
        order = jnp.sum(x_scr[mine, :].astype(F32) * cnt_scr[mine, :], axis=0, keepdims=True)
        slot = jnp.where(m[:1], kb * share + order.astype(jnp.int32), -1)
        pick = jnp.where(slot_i == slot, 1.0, 0.0).astype(BF16)
        o = mm(lhs, pick, NT)
        for t in range(planes):
            osc[t, here, :] = o[t * group:(t + 1) * group, :]
        return _

    lax.fori_loop(0, combos, weigh, 0)
    fresh_ref[...] = mm(fw_scr[...].astype(BF16), iv_ref[...])

    turned = [osc[t].T for t in range(planes)]
    if share % 8 == 0:
        for k in range(keepers):
            pieces = [t[k * share:(k + 1) * share, :] for t in turned]
            rest = w_ref.shape[1] - planes * share
            if rest:
                pieces.append(jnp.zeros((rest, rows), F32))
            w_ref[k] = jnp.concatenate(pieces, axis=0).astype(BF16)
    else:
        for t in range(planes):
            w_ref[t] = turned[t].astype(BF16)


def owner(length, q, nk, iv, kl, rk, sm, ch, share, n, pool):
    tokens, rank = kl.shape
    heads, blocks = sm.shape
    combos, n_sel = ch.shape
    rows = q.shape[0]
    slots = n * share
    planes = BLOCK_TOKENS + 1
    wire = -(-planes * share // 16) * 16
    base, off = rope_tables(blocks)
    pairs = heads // 2
    direct = share % 8 == 0
    w_shape = (n, wire, rows) if direct else (planes, slots, rows)
    vmem = pl.BlockSpec(memory_space=pltpu.VMEM)
    w, fresh = pl.pallas_call(
        functools.partial(owner_kernel, share, pool),
        out_shape=(jax.ShapeDtypeStruct(w_shape, BF16), jax.ShapeDtypeStruct((rows, HEAD_SIZE), F32)),
        in_specs=[pl.BlockSpec(memory_space=pltpu.SMEM)] + [vmem] * 9,
        out_specs=(vmem, vmem),
        scratch_shapes=[
            pltpu.VMEM((-(-rank // HEAD_SIZE), tokens, HEAD_SIZE), F32),
            pltpu.VMEM((BLOCK_TOKENS, rows, blocks), F32),
            pltpu.VMEM((pairs, -(-rank // HEAD_SIZE) * HEAD_SIZE, 2 * HEAD_SIZE), BF16),
            pltpu.VMEM((pairs, rows // pairs, 2 * HEAD_SIZE), BF16),
            pltpu.VMEM((rows, HEAD_SIZE), F32),
            pltpu.VMEM((rows, nk.shape[0]), F32),
            pltpu.VMEM((rows, 1), F32),
            pltpu.VMEM((rows, nk.shape[0]), F32),
            pltpu.VMEM((combos, 8, blocks), F32),
            pltpu.VMEM((combos * n, blocks), BF16),
            pltpu.VMEM((combos * n, blocks), F32),
            pltpu.VMEM((planes, rows, slots), F32),
        ],
        compiler_params=pltpu.CompilerParams(vmem_limit_bytes=48 * 1024 * 1024),
        name="owner",
    )(length, q, nk, iv, kl, rk, sm, ch, jnp.asarray(base), jnp.asarray(off))
    if not direct:
        w = w.reshape(planes, n, share, rows).transpose(1, 0, 2, 3).reshape(n, planes * share, rows)
        w = jnp.pad(w, ((0, 0), (0, wire - planes * share), (0, 0)))
    return w, fresh


def holder_kernel(share, combos, par_ref, w_ref, v_ref, keep_ref, send_ref, vbuf, idx_v, idx_s, vsem, isem):
    n, wire, rows = w_ref.shape
    group = rows // combos
    body = BLOCK_TOKENS * share
    fuse = max(1, min(combos, 256 // body))
    load = pltpu.make_async_copy(v_ref, vbuf, vsem)
    load.start()
    raw = w_ref[:, body:body + share, :].astype(F32).reshape(n * share, rows).astype(BF16)
    ci = lax.broadcasted_iota(jnp.int32, (combos, rows), 0)
    li = lax.broadcasted_iota(jnp.int32, (combos, rows), 1)
    sel = jnp.where(li == ci * group, 256.0, jnp.where(li == ci * group + 1, 1.0, 0.0)).astype(BF16)
    idx_v[...] = mm(sel, raw, NT).astype(jnp.int32)
    fetch = pltpu.make_async_copy(idx_v, idx_s, isem)
    fetch.start()
    width = fuse * body
    a = lax.broadcasted_iota(jnp.int32, (body, width), 0)
    b = lax.broadcasted_iota(jnp.int32, (body, width), 1) % body
    turn = jnp.where(
        jnp.logical_and(a // share == b % BLOCK_TOKENS, a % share == b // BLOCK_TOKENS), 1.0, 0.0
    ).astype(BF16)
    rc = lax.broadcasted_iota(jnp.int32, (rows, width), 0) // group
    own = (rc % fuse) == lax.broadcasted_iota(jnp.int32, (rows, width), 1) // body
    fetch.wait()
    load.wait()
    par = par_ref[0]

    def one(r):
        wt = w_ref[r, :body, :].astype(F32).T.astype(BF16)
        wide = jnp.where(own, mm(wt, turn), 0.0).astype(BF16)
        outs = []
        for g in range(combos // fuse):
            tiles = []
            for c in range(fuse):
                for i in range(share):
                    tiles.append(vbuf[idx_s[g * fuse + c, r * share + i]])
            outs.append(mm(wide[g * fuse * group:(g + 1) * fuse * group, :], jnp.concatenate(tiles, axis=0)))
        return jnp.concatenate(outs, axis=0)

    def step(m, _):
        send_ref[m] = one(2 * m + 1 - par).astype(BF16)
        keep_ref[m] = one(2 * m + par)
        return _

    lax.fori_loop(0, n // 2, step, 0)


def holder(par, w, v, share, combos):
    n, wire, rows = w.shape
    vmem = pl.BlockSpec(memory_space=pltpu.VMEM)
    return pl.pallas_call(
        functools.partial(holder_kernel, share, combos),
        out_shape=(
            jax.ShapeDtypeStruct((n // 2, rows, HEAD_SIZE), F32),
            jax.ShapeDtypeStruct((n // 2, rows, HEAD_SIZE), BF16),
        ),
        in_specs=[pl.BlockSpec(memory_space=pltpu.SMEM), vmem, pl.BlockSpec(memory_space=pl.ANY)],
        out_specs=(vmem, vmem),
        scratch_shapes=[
            pltpu.VMEM(v.shape, v.dtype),
            pltpu.VMEM((combos, n * share), jnp.int32),
            pltpu.SMEM((combos, n * share), jnp.int32),
            pltpu.SemaphoreType.DMA,
            pltpu.SemaphoreType.DMA,
        ],
        compiler_params=pltpu.CompilerParams(vmem_limit_bytes=56 * 1024 * 1024),
        name="holder",
    )(par, w, v)


def per_device(
    queries, new_keys, incoming_values, key_left, right_key_factor, value_tile_store, slot_map, chosen, lengths,
):
    n = lax.axis_size("store")
    me = lax.axis_index("store")
    steps, _, heads, n_sel = chosen.shape
    blocks = slot_map.shape[2]
    combos = steps * heads
    share = max(1, blocks // n // 4)
    pool = value_tile_store.shape[0]
    q = queries.reshape(-1, HEAD_SIZE)
    w, fresh = owner(
        lengths, q, new_keys.reshape(-1, HEAD_SIZE), incoming_values.reshape(-1, HEAD_SIZE), key_left[0],
        right_key_factor[0], slot_map[0], chosen.reshape(combos, n_sel), share, n, pool,
    )
    w, store = lax.optimization_barrier((w, value_tile_store))
    tiles = store.reshape(pool, BLOCK_TOKENS, HEAD_SIZE)
    w = lax.all_to_all(w, "store", split_axis=0, concat_axis=0, tiled=True)
    par = (me % 2).astype(jnp.int32).reshape(1)
    keep, send = holder(par, w, tiles, share, combos)
    other = lax.ppermute(send, "store", [(i, i ^ 1) for i in range(n)])
    both = (keep + other.astype(F32)).astype(BF16)
    groups = [[i for i in range(n) if i % 2 == c] for c in range(2)]
    parts = lax.all_to_all(both, "store", split_axis=0, concat_axis=0, tiled=True, axis_index_groups=groups)
    out = fresh + jnp.sum(parts.astype(F32), axis=0)
    return out.astype(BF16).reshape(queries.shape)


def solution(mesh):
    in_specs = (
        P(None, ("groups", "store"), None),
        P(None, ("groups", "store"), None),
        P(None, ("groups", "store"), None),
        P(("groups", "store"), None, None),
        P(("groups", "store"), None, None),
        P(("groups", "store"), None),
        P(("groups", "store"), None, None),
        P(None, ("groups", "store"), None, None),
        P(("groups", "store")),
    )
    out_specs = P(None, ("groups", "store"), None)
    return jax.shard_map(
        per_device, mesh=mesh, in_specs=in_specs, out_specs=out_specs, check_vma=False
    )
```

```python
import functools

import jax
import jax.numpy as jnp
import numpy as np
from jax import lax
from jax.experimental import pallas as pl
from jax.experimental.pallas import tpu as pltpu
from jax.sharding import PartitionSpec as P

HEAD_SIZE = 128
HALF = HEAD_SIZE // 2
BLOCK_TOKENS = 8
LANES = 128
ROPE_BASE = 500000.0
NT = (((1,), (1,)), ((), ()))
NN = (((1,), (0,)), ((), ()))
F32 = jnp.float32
BF16 = jnp.bfloat16


def mm(a, b, dims=NN):
    return lax.dot_general(a, b, dims, preferred_element_type=F32)


def rope_tables(blocks):
    exponent = -(np.arange(HALF, dtype=np.float32) * np.float32(2.0) / np.float32(HEAD_SIZE))
    freq = np.float32(ROPE_BASE) ** exponent
    pos = np.arange(blocks * BLOCK_TOKENS).reshape(-1, LANES, BLOCK_TOKENS).transpose(0, 2, 1)
    pos = pos.reshape(-1, 2 * LANES).astype(np.float32)
    angle = (pos[:, None, :] * freq[None, :, None]).astype(np.float64)
    keys = np.stack([np.cos(angle), np.sin(angle)], axis=1).astype(np.float32)
    freq = np.concatenate([freq, freq]).astype(np.float64)
    rows = np.arange(-(-(blocks + 2) // 8) * 8, dtype=np.float64)[:, None] * BLOCK_TOKENS
    offs = np.arange(BLOCK_TOKENS, dtype=np.float64)[:, None]
    base = np.stack([np.cos(rows * freq), np.sin(rows * freq)]).astype(np.float32)
    off = np.stack([np.cos(offs * freq), np.sin(offs * freq)]).astype(np.float32)
    return keys, base, off


def split3(x):
    a = x.astype(BF16)
    r = x - a.astype(F32)
    b = r.astype(BF16)
    return a, b, (r - b.astype(F32)).astype(BF16)


def owner_kernel(
    share, pool, keepers, len_ref, q_hbm, nk_hbm, iv_hbm, kl_hbm, rk_hbm, sm_hbm, ch_hbm, tab_hbm, base_hbm, off_hbm,
    w_ref, fresh_ref,
    q_ref, nk_ref, iv_ref, kl_ref, rk_ref, sm_ref, ch_ref, tab_ref, base_ref, off_ref, sems,
    lp, kk, rt, qp, qr, nr, vr, sc, fs_scr, fm_scr, fw_scr, pm, osc,
):
    rank, tokens = kl_ref.shape
    heads, blocks = sm_ref.shape
    combos, n_sel = ch_ref.shape
    steps = combos // heads
    rows = qr.shape[0]
    group = rows // combos
    planes = osc.shape[0]
    slots = osc.shape[2]
    pairs = heads // 2
    per_step = heads * group
    chunks = blocks // LANES
    scale = HEAD_SIZE ** -0.5
    length = len_ref[0]

    moves = []
    for i, (src, dst) in enumerate((
        (kl_hbm, kl_ref), (rk_hbm, rk_ref), (q_hbm, q_ref), (nk_hbm, nk_ref), (iv_hbm, iv_ref), (sm_hbm, sm_ref),
        (ch_hbm, ch_ref), (base_hbm, base_ref), (off_hbm, off_ref), (tab_hbm, tab_ref),
    )):
        move = pltpu.make_async_copy(src, dst, sems.at[i])
        move.start()
        moves.append(move)

    lane = lax.broadcasted_iota(jnp.int32, (1, HEAD_SIZE), 1)
    low = lane < HALF
    half = 4 * LANES
    to = lax.broadcasted_iota(jnp.int32, (1, half), 1)
    pm[...] = jnp.where(
        lax.broadcasted_iota(jnp.int32, (half, half), 0) == (to % HALF) * BLOCK_TOKENS + to // HALF, 1.0, 0.0
    ).astype(BF16)

    for move in moves[:2]:
        move.wait()

    def order(i, _):
        at = pl.multiple_of(i * 2 * half, 2 * half)
        a = mm(kl_ref[:, pl.ds(at, half)], pm[...])
        b = mm(kl_ref[:, pl.ds(at + half, half)], pm[...])
        for m in range(BLOCK_TOKENS // 2):
            x = a[:, m * LANES:(m + 1) * LANES]
            y = b[:, m * LANES:(m + 1) * LANES]
            even = jnp.where(low, x, pltpu.roll(y, HALF, 1))
            odd = jnp.where(low, pltpu.roll(x, HALF, 1), y)
            lp[i * (BLOCK_TOKENS // 2) + m] = jnp.concatenate([even, odd], axis=1).astype(BF16)
        return _

    lax.fori_loop(0, chunks, order, 0)
    for h in range(heads):
        rt[h * HEAD_SIZE:(h + 1) * HEAD_SIZE, :] = (
            rk_ref[:, h * HEAD_SIZE:(h + 1) * HEAD_SIZE].astype(F32).T.astype(BF16)
        )

    for move in moves[2:9]:
        move.wait()
    x = q_ref[...].astype(F32)
    for k in range(per_step):
        qr[pl.ds(k, steps, stride=per_step), :] = x[:, k * HEAD_SIZE:(k + 1) * HEAD_SIZE]
    x = nk_ref[...].astype(F32)
    y = iv_ref[...].astype(F32)
    for k in range(heads):
        nr[pl.ds(k, steps, stride=heads), :] = x[:, k * HEAD_SIZE:(k + 1) * HEAD_SIZE]
        vr[pl.ds(k, steps, stride=heads), :] = y[:, k * HEAD_SIZE:(k + 1) * HEAD_SIZE]

    sign = jnp.where(low, -1.0, 1.0).astype(F32)

    def angle(position):
        b = position // BLOCK_TOKENS
        j = position - b * BLOCK_TOKENS
        cb = base_ref[0, pl.ds(b, 1), :]
        sb = base_ref[1, pl.ds(b, 1), :]
        cj = off_ref[0, pl.ds(j, 1), :]
        sj = off_ref[1, pl.ds(j, 1), :]
        return cb * cj - sb * sj, (sb * cj + cb * sj) * sign

    fresh_keys = []
    for s in range(steps):
        c, sn = angle(length + s)
        x = qr[s * per_step:(s + 1) * per_step, :]
        x = x * c + pltpu.roll(x, HALF, 1) * sn
        qr[s * per_step:(s + 1) * per_step, :] = x.astype(BF16).astype(F32)
        y = nr[s * heads:(s + 1) * heads, :]
        fresh_keys.append(y * c + pltpu.roll(y, HALF, 1) * sn)
    fk = jnp.concatenate(fresh_keys, axis=0).astype(BF16)
    fs = mm(qr[...].astype(BF16), fk, NT) * scale
    ri = lax.broadcasted_iota(jnp.int32, fs.shape, 0)
    ci = lax.broadcasted_iota(jnp.int32, fs.shape, 1)
    keep = jnp.logical_and((ri // group) % heads == ci % heads, ci // heads <= ri // per_step)
    fs = jnp.where(keep, fs, -jnp.inf)
    fs_scr[...] = fs
    fm_scr[...] = jnp.max(fs, axis=1, keepdims=True)

    for p in range(pairs):
        pieces = []
        for s in range(steps):
            for hh in range(2):
                start = s * per_step + (2 * p + hh) * group
                x = qr[start:start + group, :]
                z = jnp.zeros_like(x)
                pieces.append(jnp.concatenate([x, z] if hh == 0 else [z, x], axis=1))
        qp[p] = jnp.concatenate(pieces, axis=0).astype(BF16)

    moves[9].wait()

    def keys(i, _):
        ct = tab_ref[i, 0]
        st = tab_ref[i, 1]
        raw = mm(rt[...], lp[i])
        for h in range(heads):
            a = raw[h * HEAD_SIZE:h * HEAD_SIZE + HALF, :]
            c = raw[h * HEAD_SIZE + HALF:(h + 1) * HEAD_SIZE, :]
            kk[i, h * HEAD_SIZE:(h + 1) * HEAD_SIZE, :] = jnp.concatenate(
                [a * ct - c * st, c * ct + a * st], axis=0
            ).astype(BF16)
        return _

    lax.fori_loop(0, lp.shape[0], keys, 0, unroll=4)

    def scores(i, _):
        at = i // (BLOCK_TOKENS // 2)
        j = 2 * (i % (BLOCK_TOKENS // 2))
        for p in range(pairs):
            out = mm(qp[p], kk[i, 2 * p * HEAD_SIZE:2 * (p + 1) * HEAD_SIZE, :]) * scale
            for s in range(steps):
                to_rows = slice(s * per_step + 2 * p * group, s * per_step + 2 * (p + 1) * group)
                for jj in range(2):
                    sc[at, j + jj, to_rows, :] = out[s * 2 * group:(s + 1) * 2 * group, jj * LANES:(jj + 1) * LANES]
        return _

    lax.fori_loop(0, lp.shape[0], scores, 0, unroll=4)

    wide = steps * n_sel
    entry = lax.broadcasted_iota(jnp.int32, (1, wide), 1)
    block_i = lax.broadcasted_iota(jnp.int32, (blocks, wide), 0)
    keeper_i = lax.broadcasted_iota(jnp.int32, (keepers, wide), 0)
    slot_i = lax.broadcasted_iota(jnp.int32, (steps * slots, wide), 0)
    e0 = lax.broadcasted_iota(jnp.int32, (wide, wide), 0)
    e1 = lax.broadcasted_iota(jnp.int32, (wide, wide), 1)
    before = jnp.where(jnp.logical_and(e0 // n_sel == e1 // n_sel, e0 < e1), 1.0, 0.0).astype(BF16)
    sub = lax.broadcasted_iota(jnp.int32, (16, blocks), 0)
    sub_e = lax.broadcasted_iota(jnp.int32, (8, wide), 0)

    def weigh(h, _):
        picked = jnp.concatenate([ch_ref[pl.ds(s * heads + h, 1), :] for s in range(steps)], axis=1)
        hot = jnp.where(block_i == picked, 1.0, 0.0).astype(BF16)
        row = sm_ref[pl.ds(h, 1), :]
        kb = row // pool
        inside = row - kb * pool
        hi = inside // 256
        lo = inside - hi * 256
        extra = jnp.where(sub == 0, hi, jnp.where(sub == 1, lo, jnp.where(sub == 2, kb, 0))).astype(F32).astype(BF16)
        got = mm(extra, hot)
        kb = got[2:3, :].astype(jnp.int32)
        kh = jnp.where(keeper_i == kb, 1.0, 0.0)
        rank_e = jnp.sum(kh * mm(kh.astype(BF16), before), axis=0, keepdims=True)
        slot = kb * share + rank_e.astype(jnp.int32) + (entry // n_sel) * slots
        pick = jnp.where(slot_i == slot, 1.0, 0.0).astype(BF16)
        xs = None
        heres = []
        for s in range(steps):
            here = pl.ds(pl.multiple_of((s * heads + h) * group, group), group)
            heres.append(here)
            x = jnp.concatenate(
                [jnp.concatenate([sc[t, j, here, :] for t in range(chunks)], axis=1) for j in range(BLOCK_TOKENS)],
                axis=0,
            )
            g = mm(jnp.concatenate(split3(x), axis=0), hot)
            size = BLOCK_TOKENS * group
            g = (g[:size] + g[size:2 * size]) + g[2 * size:]
            xs = g if xs is None else jnp.where(entry // n_sel == s, g, xs)
        pos = picked * BLOCK_TOKENS
        xs = [
            jnp.where(pos + j < length, xs[j * group:(j + 1) * group, :], -jnp.inf) for j in range(BLOCK_TOKENS)
        ]
        most = functools.reduce(jnp.maximum, xs)
        tops = []
        top = None
        for s in range(steps):
            mine = entry // n_sel == s
            t = jnp.max(jnp.where(mine, most, -jnp.inf), axis=1, keepdims=True)
            t = jnp.maximum(t, fm_scr[heres[s], :])
            tops.append(t)
            top = jnp.broadcast_to(t, most.shape) if top is None else jnp.where(mine, t, top)
        es = [jnp.exp(x - top) for x in xs]
        added = functools.reduce(jnp.add, es)
        inv = None
        for s in range(steps):
            mine = entry // n_sel == s
            fe = jnp.exp(fs_scr[heres[s], :] - tops[s])
            total = jnp.sum(jnp.where(mine, added, 0.0), axis=1, keepdims=True)
            one = 1.0 / (total + jnp.sum(fe, axis=1, keepdims=True))
            fw_scr[heres[s], :] = fe * one
            inv = jnp.broadcast_to(one, most.shape) if inv is None else jnp.where(mine, one, inv)
        tail = jnp.where(sub_e < 2, got[:8, :], 0.0)
        lhs = jnp.concatenate([e * inv for e in es] + [tail, jnp.zeros_like(tail)], axis=0).astype(BF16)
        o = mm(lhs, pick, NT)
        for t in range(planes):
            for s in range(steps):
                osc[t, heres[s], :] = o[t * group:(t + 1) * group, s * slots:(s + 1) * slots]
        return _

    lax.fori_loop(0, heads, weigh, 0, unroll=2)
    fresh_ref[...] = mm(fw_scr[...].astype(BF16), vr[...].astype(BF16))

    turned = [osc[t].T for t in range(planes)]
    if share % 8 == 0:
        for k in range(keepers):
            w_ref[k] = jnp.concatenate([t[k * share:(k + 1) * share, :] for t in turned], axis=0).astype(BF16)
    else:
        for t in range(planes):
            w_ref[t] = turned[t].astype(BF16)


def owner(length, q, nk, iv, kl, rk, sm, ch, share, n, pool):
    rank, tokens = kl.shape
    heads, blocks = sm.shape
    combos, n_sel = ch.shape
    rows = q.size // HEAD_SIZE
    fresh_rows = nk.size // HEAD_SIZE
    slots = n * share
    planes = BLOCK_TOKENS + 1
    pairs = heads // 2
    direct = share % 8 == 0
    w_shape = (n, planes * share, rows) if direct else (planes, slots, rows)
    hbm = pl.BlockSpec(memory_space=pl.ANY)
    vmem = pl.BlockSpec(memory_space=pltpu.VMEM)
    operands = (q, nk, iv, kl, rk, sm, ch) + tuple(jnp.asarray(t) for t in rope_tables(blocks))
    w, fresh = pl.pallas_call(
        functools.partial(owner_kernel, share, pool, n),
        out_shape=(jax.ShapeDtypeStruct(w_shape, BF16), jax.ShapeDtypeStruct((rows, HEAD_SIZE), F32)),
        in_specs=[pl.BlockSpec(memory_space=pltpu.SMEM)] + [hbm] * len(operands),
        out_specs=(vmem, vmem),
        scratch_shapes=[pltpu.VMEM(x.shape, x.dtype) for x in operands] + [
            pltpu.SemaphoreType.DMA((len(operands),)),
            pltpu.VMEM((tokens // (2 * LANES), rank, 2 * LANES), BF16),
            pltpu.VMEM((tokens // (2 * LANES), heads * HEAD_SIZE, 2 * LANES), BF16),
            pltpu.VMEM((heads * HEAD_SIZE, rank), BF16),
            pltpu.VMEM((pairs, rows // pairs, 2 * HEAD_SIZE), BF16),
            pltpu.VMEM((rows, HEAD_SIZE), F32),
            pltpu.VMEM((fresh_rows, HEAD_SIZE), F32),
            pltpu.VMEM((fresh_rows, HEAD_SIZE), F32),
            pltpu.VMEM((blocks // LANES, BLOCK_TOKENS, rows, LANES), F32),
            pltpu.VMEM((rows, fresh_rows), F32),
            pltpu.VMEM((rows, 1), F32),
            pltpu.VMEM((rows, fresh_rows), F32),
            pltpu.VMEM((4 * LANES, 4 * LANES), BF16),
            pltpu.VMEM((planes, rows, slots), F32),
        ],
        compiler_params=pltpu.CompilerParams(vmem_limit_bytes=60 * 1024 * 1024),
        name="owner",
    )(length, *operands)
    if not direct:
        w = w.reshape(planes, n, share, rows).transpose(1, 0, 2, 3).reshape(n, planes * share, rows)
    return w, fresh


def holder_kernel(share, combos, par_ref, w_ref, v_ref, keep_ref, send_ref, idx_v, idx_s, isem):
    n, wire, rows = w_ref.shape
    group = rows // combos
    body = BLOCK_TOKENS * share
    fuse = max(1, min(combos, 256 // body))
    raw = w_ref[:, body:body + share, :].astype(F32).reshape(n * share, rows).astype(BF16)
    ci = lax.broadcasted_iota(jnp.int32, (combos, rows), 0)
    li = lax.broadcasted_iota(jnp.int32, (combos, rows), 1)
    sel = jnp.where(li == ci * group, 256.0, jnp.where(li == ci * group + 1, 1.0, 0.0)).astype(BF16)
    idx_v[...] = mm(sel, raw, NT).astype(jnp.int32)
    fetch = pltpu.make_async_copy(idx_v, idx_s, isem)
    fetch.start()
    width = fuse * body
    a = lax.broadcasted_iota(jnp.int32, (body, width), 0)
    b = lax.broadcasted_iota(jnp.int32, (body, width), 1) % body
    turn = jnp.where(
        jnp.logical_and(a // share == b % BLOCK_TOKENS, a % share == b // BLOCK_TOKENS), 1.0, 0.0
    ).astype(BF16)
    rc = lax.broadcasted_iota(jnp.int32, (rows, width), 0) // group
    own = (rc % fuse) == lax.broadcasted_iota(jnp.int32, (rows, width), 1) // body
    fetch.wait()
    par = par_ref[0]

    def one(r):
        wt = w_ref[r, :body, :].astype(F32).T.astype(BF16)
        wide = jnp.where(own, mm(wt, turn), 0.0).astype(BF16)
        outs = []
        for g in range(combos // fuse):
            tiles = []
            for c in range(fuse):
                for i in range(share):
                    tiles.append(v_ref[idx_s[g * fuse + c, r * share + i]])
            outs.append(mm(wide[g * fuse * group:(g + 1) * fuse * group, :], jnp.concatenate(tiles, axis=0)))
        return jnp.concatenate(outs, axis=0)

    def step(m, _):
        send_ref[m] = one(2 * m + 1 - par).astype(BF16)
        keep_ref[m] = one(2 * m + par)
        return _

    lax.fori_loop(0, n // 2, step, 0)


def holder(par, w, v, share, combos):
    n, wire, rows = w.shape
    vmem = pl.BlockSpec(memory_space=pltpu.VMEM)
    return pl.pallas_call(
        functools.partial(holder_kernel, share, combos),
        out_shape=(
            jax.ShapeDtypeStruct((n // 2, rows, HEAD_SIZE), F32),
            jax.ShapeDtypeStruct((n // 2, rows, HEAD_SIZE), BF16),
        ),
        in_specs=[pl.BlockSpec(memory_space=pltpu.SMEM), vmem, vmem],
        out_specs=(vmem, vmem),
        scratch_shapes=[
            pltpu.VMEM((combos, n * share), jnp.int32),
            pltpu.SMEM((combos, n * share), jnp.int32),
            pltpu.SemaphoreType.DMA,
        ],
        compiler_params=pltpu.CompilerParams(vmem_limit_bytes=20 * 1024 * 1024),
        name="holder",
    )(par, w, v)


def per_device(
    queries, new_keys, incoming_values, key_left, right_key_factor, value_tile_store, slot_map, chosen, lengths,
):
    n = lax.axis_size("store")
    me = lax.axis_index("store")
    steps, _, heads, n_sel = chosen.shape
    blocks = slot_map.shape[2]
    combos = steps * heads
    share = max(1, blocks // n // 4)
    pool = value_tile_store.shape[0]
    w, fresh = owner(
        lengths, queries[:, 0], new_keys[:, 0], incoming_values[:, 0], key_left[0].T,
        right_key_factor[0], slot_map[0], chosen.reshape(combos, n_sel), share, n, pool,
    )
    w, store = lax.optimization_barrier((w, value_tile_store))
    tiles = store.reshape(pool, BLOCK_TOKENS, HEAD_SIZE)
    w = lax.all_to_all(w, "store", split_axis=0, concat_axis=0, tiled=True)
    par = (me % 2).astype(jnp.int32).reshape(1)
    keep, send = holder(par, w, tiles, share, combos)
    other = lax.ppermute(send, "store", [(i, i ^ 1) for i in range(n)])
    both = (keep + other.astype(F32)).astype(BF16)
    groups = [[i for i in range(n) if i % 2 == c] for c in range(2)]
    parts = lax.all_to_all(both, "store", split_axis=0, concat_axis=0, tiled=True, axis_index_groups=groups)
    out = fresh + jnp.sum(parts.astype(F32), axis=0)
    return out.astype(BF16).reshape(queries.shape)


def solution(mesh):
    in_specs = (
        P(None, ("groups", "store"), None),
        P(None, ("groups", "store"), None),
        P(None, ("groups", "store"), None),
        P(("groups", "store"), None, None),
        P(("groups", "store"), None, None),
        P(("groups", "store"), None),
        P(("groups", "store"), None, None),
        P(None, ("groups", "store"), None, None),
        P(("groups", "store")),
    )
    out_specs = P(None, ("groups", "store"), None)
    return jax.shard_map(
        per_device, mesh=mesh, in_specs=in_specs, out_specs=out_specs, check_vma=False
    )
```

```python
import functools

import jax
import jax.numpy as jnp
import numpy as np
from jax import lax
from jax.experimental import pallas as pl
from jax.experimental.pallas import tpu as pltpu
from jax.sharding import PartitionSpec as P

HEAD_SIZE = 128
HALF = HEAD_SIZE // 2
BLOCK_TOKENS = 8
LANES = 128
ROPE_BASE = 500000.0
NT = (((1,), (1,)), ((), ()))
NN = (((1,), (0,)), ((), ()))
F32 = jnp.float32
BF16 = jnp.bfloat16


def mm(a, b, dims=NN):
    return lax.dot_general(a, b, dims, preferred_element_type=F32)


def rope_tables(blocks):
    exponent = -(np.arange(HALF, dtype=np.float32) * np.float32(2.0) / np.float32(HEAD_SIZE))
    freq = np.float32(ROPE_BASE) ** exponent
    pos = np.arange(blocks * BLOCK_TOKENS).reshape(-1, LANES, BLOCK_TOKENS).transpose(0, 2, 1)
    pos = pos.reshape(-1, 2 * LANES).astype(np.float32)
    angle = (pos[:, None, :] * freq[None, :, None]).astype(np.float64)
    keys = np.stack([np.cos(angle), np.sin(angle)], axis=1).astype(np.float32)
    freq = np.concatenate([freq, freq]).astype(np.float64)
    rows = np.arange(-(-(blocks + 2) // 8) * 8, dtype=np.float64)[:, None] * BLOCK_TOKENS
    offs = np.arange(BLOCK_TOKENS, dtype=np.float64)[:, None]
    base = np.stack([np.cos(rows * freq), np.sin(rows * freq)]).astype(np.float32)
    off = np.stack([np.cos(offs * freq), np.sin(offs * freq)]).astype(np.float32)
    return keys, base, off


def split3(x):
    a = x.astype(BF16)
    r = x - a.astype(F32)
    b = r.astype(BF16)
    return a, b, (r - b.astype(F32)).astype(BF16)


def owner_kernel(
    share, pool, keepers, len_ref, q_hbm, nk_hbm, iv_hbm, kl_hbm, rk_hbm, sm_hbm, ch_hbm, tab_hbm, base_hbm, off_hbm,
    w_ref, fresh_ref,
    q_ref, nk_ref, iv_ref, kl_ref, rk_ref, sm_ref, ch_ref, tab_ref, base_ref, off_ref, sems,
    lp, kk, rt, qp, qr, nr, vr, sc, fs_scr, fm_scr, fw_scr, pm, osc,
):
    rank, tokens = kl_ref.shape
    heads, blocks = sm_ref.shape
    combos, n_sel = ch_ref.shape
    steps = combos // heads
    rows = qr.shape[0]
    group = rows // combos
    planes = osc.shape[0]
    slots = osc.shape[2]
    pairs = heads // 2
    per_step = heads * group
    chunks = blocks // LANES
    scale = HEAD_SIZE ** -0.5
    length = len_ref[0]

    half = 4 * LANES
    count = [0]

    def bring(src, dst):
        move = pltpu.make_async_copy(src, dst, sems.at[count[0]])
        move.start()
        count[0] += 1
        return move

    lefts = []
    for t in range(chunks):
        at = slice(t * 2 * half, (t + 1) * 2 * half)
        lefts.append(bring(kl_hbm.at[:, at], kl_ref.at[:, at]))
    right = bring(rk_hbm, rk_ref)
    small = [bring(*x) for x in (
        (q_hbm, q_ref), (nk_hbm, nk_ref), (iv_hbm, iv_ref), (sm_hbm, sm_ref), (ch_hbm, ch_ref),
        (base_hbm, base_ref), (off_hbm, off_ref),
    )]
    per_chunk = BLOCK_TOKENS // 2
    tables = []
    for t in range(chunks):
        at = slice(t * per_chunk, (t + 1) * per_chunk)
        tables.append(bring(tab_hbm.at[at], tab_ref.at[at]))

    lane = lax.broadcasted_iota(jnp.int32, (1, HEAD_SIZE), 1)
    low = lane < HALF
    to = lax.broadcasted_iota(jnp.int32, (1, half), 1)
    pm[...] = jnp.where(
        lax.broadcasted_iota(jnp.int32, (half, half), 0) == (to % HALF) * BLOCK_TOKENS + to // HALF, 1.0, 0.0
    ).astype(BF16)

    for i in range(chunks):
        lefts[i].wait()
        at = i * 2 * half
        a = mm(kl_ref[:, at:at + half], pm[...])
        b = mm(kl_ref[:, at + half:at + 2 * half], pm[...])
        for m in range(BLOCK_TOKENS // 2):
            x = a[:, m * LANES:(m + 1) * LANES]
            y = b[:, m * LANES:(m + 1) * LANES]
            even = jnp.where(low, x, pltpu.roll(y, HALF, 1))
            odd = jnp.where(low, pltpu.roll(x, HALF, 1), y)
            lp[i * per_chunk + m] = jnp.concatenate([even, odd], axis=1).astype(BF16)

    right.wait()
    for h in range(heads):
        rt[h * HEAD_SIZE:(h + 1) * HEAD_SIZE, :] = (
            rk_ref[:, h * HEAD_SIZE:(h + 1) * HEAD_SIZE].astype(F32).T.astype(BF16)
        )

    for move in small:
        move.wait()
    x = q_ref[...].astype(F32)
    for k in range(per_step):
        qr[pl.ds(k, steps, stride=per_step), :] = x[:, k * HEAD_SIZE:(k + 1) * HEAD_SIZE]
    x = nk_ref[...].astype(F32)
    y = iv_ref[...].astype(F32)
    for k in range(heads):
        nr[pl.ds(k, steps, stride=heads), :] = x[:, k * HEAD_SIZE:(k + 1) * HEAD_SIZE]
        vr[pl.ds(k, steps, stride=heads), :] = y[:, k * HEAD_SIZE:(k + 1) * HEAD_SIZE]

    sign = jnp.where(low, -1.0, 1.0).astype(F32)

    def angle(position):
        b = position // BLOCK_TOKENS
        j = position - b * BLOCK_TOKENS
        cb = base_ref[0, pl.ds(b, 1), :]
        sb = base_ref[1, pl.ds(b, 1), :]
        cj = off_ref[0, pl.ds(j, 1), :]
        sj = off_ref[1, pl.ds(j, 1), :]
        return cb * cj - sb * sj, (sb * cj + cb * sj) * sign

    fresh_keys = []
    for s in range(steps):
        c, sn = angle(length + s)
        x = qr[s * per_step:(s + 1) * per_step, :]
        x = x * c + pltpu.roll(x, HALF, 1) * sn
        qr[s * per_step:(s + 1) * per_step, :] = x.astype(BF16).astype(F32)
        y = nr[s * heads:(s + 1) * heads, :]
        fresh_keys.append(y * c + pltpu.roll(y, HALF, 1) * sn)
    fk = jnp.concatenate(fresh_keys, axis=0).astype(BF16)
    fs = mm(qr[...].astype(BF16), fk, NT) * scale
    ri = lax.broadcasted_iota(jnp.int32, fs.shape, 0)
    ci = lax.broadcasted_iota(jnp.int32, fs.shape, 1)
    keep = jnp.logical_and((ri // group) % heads == ci % heads, ci // heads <= ri // per_step)
    fs = jnp.where(keep, fs, -jnp.inf)
    fs_scr[...] = fs
    fm_scr[...] = jnp.max(fs, axis=1, keepdims=True)

    for p in range(pairs):
        pieces = []
        for s in range(steps):
            for hh in range(2):
                start = s * per_step + (2 * p + hh) * group
                x = qr[start:start + group, :]
                z = jnp.zeros_like(x)
                pieces.append(jnp.concatenate([x, z] if hh == 0 else [z, x], axis=1))
        qp[p] = jnp.concatenate(pieces, axis=0).astype(BF16)

    def keys(i):
        ct = tab_ref[i, 0]
        st = tab_ref[i, 1]
        raw = mm(rt[...], lp[i])
        for h in range(heads):
            a = raw[h * HEAD_SIZE:h * HEAD_SIZE + HALF, :]
            c = raw[h * HEAD_SIZE + HALF:(h + 1) * HEAD_SIZE, :]
            kk[i, h * HEAD_SIZE:(h + 1) * HEAD_SIZE, :] = jnp.concatenate(
                [a * ct - c * st, c * ct + a * st], axis=0
            ).astype(BF16)

    for t in range(chunks):
        tables[t].wait()
        for i in range(t * per_chunk, (t + 1) * per_chunk):
            keys(i)

    def scores(i):
        at = i // per_chunk
        j = 2 * (i % per_chunk)
        for p in range(pairs):
            out = mm(qp[p], kk[i, 2 * p * HEAD_SIZE:2 * (p + 1) * HEAD_SIZE, :]) * scale
            for s in range(steps):
                to_rows = slice(s * per_step + 2 * p * group, s * per_step + 2 * (p + 1) * group)
                for jj in range(2):
                    sc[at, j + jj, to_rows, :] = out[s * 2 * group:(s + 1) * 2 * group, jj * LANES:(jj + 1) * LANES]

    for i in range(lp.shape[0]):
        scores(i)

    wide = steps * n_sel
    entry = lax.broadcasted_iota(jnp.int32, (1, wide), 1)
    block_i = lax.broadcasted_iota(jnp.int32, (blocks, wide), 0)
    keeper_i = lax.broadcasted_iota(jnp.int32, (keepers, wide), 0)
    slot_i = lax.broadcasted_iota(jnp.int32, (steps * slots, wide), 0)
    e0 = lax.broadcasted_iota(jnp.int32, (wide, wide), 0)
    e1 = lax.broadcasted_iota(jnp.int32, (wide, wide), 1)
    before = jnp.where(jnp.logical_and(e0 // n_sel == e1 // n_sel, e0 < e1), 1.0, 0.0).astype(BF16)
    sub = lax.broadcasted_iota(jnp.int32, (16, blocks), 0)
    sub_e = lax.broadcasted_iota(jnp.int32, (8, wide), 0)

    def weigh(h):
        picked = jnp.concatenate([ch_ref[s * heads + h:s * heads + h + 1, :] for s in range(steps)], axis=1)
        hot = jnp.where(block_i == picked, 1.0, 0.0).astype(BF16)
        row = sm_ref[h:h + 1, :]
        kb = row // pool
        inside = row - kb * pool
        hi = inside // 256
        lo = inside - hi * 256
        extra = jnp.where(sub == 0, hi, jnp.where(sub == 1, lo, jnp.where(sub == 2, kb, 0))).astype(F32).astype(BF16)
        terms = [extra]
        heres = []
        for s in range(steps):
            here = slice((s * heads + h) * group, (s * heads + h + 1) * group)
            heres.append(here)
            x = jnp.concatenate(
                [jnp.concatenate([sc[t, j, here, :] for t in range(chunks)], axis=1) for j in range(BLOCK_TOKENS)],
                axis=0,
            )
            terms += split3(x)
        got = mm(jnp.concatenate(terms, axis=0), hot)
        kb = got[2:3, :].astype(jnp.int32)
        kh = jnp.where(keeper_i == kb, 1.0, 0.0)
        rank_e = jnp.sum(kh * mm(kh.astype(BF16), before), axis=0, keepdims=True)
        slot = kb * share + rank_e.astype(jnp.int32) + (entry // n_sel) * slots
        pick = jnp.where(slot_i == slot, 1.0, 0.0).astype(BF16)
        xs = None
        size = BLOCK_TOKENS * group
        for s in range(steps):
            at = extra.shape[0] + 3 * s * size
            g = (got[at:at + size] + got[at + size:at + 2 * size]) + got[at + 2 * size:at + 3 * size]
            xs = g if xs is None else jnp.where(entry // n_sel == s, g, xs)
        pos = picked * BLOCK_TOKENS
        xs = [
            jnp.where(pos + j < length, xs[j * group:(j + 1) * group, :], -jnp.inf) for j in range(BLOCK_TOKENS)
        ]
        most = functools.reduce(jnp.maximum, xs)
        tops = []
        top = None
        for s in range(steps):
            mine = entry // n_sel == s
            t = jnp.max(jnp.where(mine, most, -jnp.inf), axis=1, keepdims=True)
            t = jnp.maximum(t, fm_scr[heres[s], :])
            tops.append(t)
            top = jnp.broadcast_to(t, most.shape) if top is None else jnp.where(mine, t, top)
        es = [jnp.exp(x - top) for x in xs]
        added = functools.reduce(jnp.add, es)
        inv = None
        for s in range(steps):
            mine = entry // n_sel == s
            fe = jnp.exp(fs_scr[heres[s], :] - tops[s])
            total = jnp.sum(jnp.where(mine, added, 0.0), axis=1, keepdims=True)
            one = 1.0 / (total + jnp.sum(fe, axis=1, keepdims=True))
            fw_scr[heres[s], :] = fe * one
            inv = jnp.broadcast_to(one, most.shape) if inv is None else jnp.where(mine, one, inv)
        tail = jnp.where(sub_e < 2, got[:8, :], 0.0)
        lhs = jnp.concatenate([e * inv for e in es] + [tail, jnp.zeros_like(tail)], axis=0).astype(BF16)
        o = mm(lhs, pick, NT)
        for t in range(planes):
            for s in range(steps):
                osc[t, heres[s], :] = o[t * group:(t + 1) * group, s * slots:(s + 1) * slots]

    for h in range(heads):
        weigh(h)
    fresh_ref[...] = mm(fw_scr[...].astype(BF16), vr[...].astype(BF16))

    turned = [osc[t].T for t in range(planes)]
    if share % 8 == 0:
        for k in range(keepers):
            w_ref[k] = jnp.concatenate([t[k * share:(k + 1) * share, :] for t in turned], axis=0).astype(BF16)
    else:
        for t in range(planes):
            w_ref[t] = turned[t].astype(BF16)


def owner(length, q, nk, iv, kl, rk, sm, ch, share, n, pool):
    rank, tokens = kl.shape
    heads, blocks = sm.shape
    combos, n_sel = ch.shape
    rows = q.size // HEAD_SIZE
    fresh_rows = nk.size // HEAD_SIZE
    slots = n * share
    planes = BLOCK_TOKENS + 1
    pairs = heads // 2
    direct = share % 8 == 0
    w_shape = (n, planes * share, rows) if direct else (planes, slots, rows)
    hbm = pl.BlockSpec(memory_space=pl.ANY)
    vmem = pl.BlockSpec(memory_space=pltpu.VMEM)
    operands = (q, nk, iv, kl, rk, sm, ch) + tuple(jnp.asarray(t) for t in rope_tables(blocks))
    w, fresh = pl.pallas_call(
        functools.partial(owner_kernel, share, pool, n),
        out_shape=(jax.ShapeDtypeStruct(w_shape, BF16), jax.ShapeDtypeStruct((rows, HEAD_SIZE), F32)),
        in_specs=[pl.BlockSpec(memory_space=pltpu.SMEM)] + [hbm] * len(operands),
        out_specs=(vmem, vmem),
        scratch_shapes=[pltpu.VMEM(x.shape, x.dtype) for x in operands] + [
            pltpu.SemaphoreType.DMA((len(operands) - 2 + 2 * (blocks // LANES),)),
            pltpu.VMEM((tokens // (2 * LANES), rank, 2 * LANES), BF16),
            pltpu.VMEM((tokens // (2 * LANES), heads * HEAD_SIZE, 2 * LANES), BF16),
            pltpu.VMEM((heads * HEAD_SIZE, rank), BF16),
            pltpu.VMEM((pairs, rows // pairs, 2 * HEAD_SIZE), BF16),
            pltpu.VMEM((rows, HEAD_SIZE), F32),
            pltpu.VMEM((fresh_rows, HEAD_SIZE), F32),
            pltpu.VMEM((fresh_rows, HEAD_SIZE), F32),
            pltpu.VMEM((blocks // LANES, BLOCK_TOKENS, rows, LANES), F32),
            pltpu.VMEM((rows, fresh_rows), F32),
            pltpu.VMEM((rows, 1), F32),
            pltpu.VMEM((rows, fresh_rows), F32),
            pltpu.VMEM((4 * LANES, 4 * LANES), BF16),
            pltpu.VMEM((planes, rows, slots), F32),
        ],
        compiler_params=pltpu.CompilerParams(vmem_limit_bytes=60 * 1024 * 1024),
        name="owner",
    )(length, *operands)
    if not direct:
        w = w.reshape(planes, n, share, rows).transpose(1, 0, 2, 3).reshape(n, planes * share, rows)
    return w, fresh


def holder_kernel(share, combos, par_ref, w_ref, v_hbm, keep_ref, send_ref, v_ref, wide, idx_v, idx_s, vsems, isem):
    n, wire, rows = w_ref.shape
    group = rows // combos
    body = BLOCK_TOKENS * share
    fuse = max(1, min(combos, 256 // body))
    parts = vsems.shape[0]
    size = v_ref.shape[0] // parts
    loads = []
    for i in range(parts):
        at = pl.ds(i * size, size)
        load = pltpu.make_async_copy(v_hbm.at[at], v_ref.at[at], vsems.at[i])
        load.start()
        loads.append(load)
    raw = w_ref[:, body:body + share, :].astype(F32).reshape(n * share, rows).astype(BF16)
    ci = lax.broadcasted_iota(jnp.int32, (combos, rows), 0)
    li = lax.broadcasted_iota(jnp.int32, (combos, rows), 1)
    sel = jnp.where(li == ci * group, 256.0, jnp.where(li == ci * group + 1, 1.0, 0.0)).astype(BF16)
    idx_v[...] = mm(sel, raw, NT).astype(jnp.int32)
    fetch = pltpu.make_async_copy(idx_v, idx_s, isem)
    fetch.start()
    width = fuse * body
    a = lax.broadcasted_iota(jnp.int32, (body, width), 0)
    b = lax.broadcasted_iota(jnp.int32, (body, width), 1) % body
    turn = jnp.where(
        jnp.logical_and(a // share == b % BLOCK_TOKENS, a % share == b // BLOCK_TOKENS), 1.0, 0.0
    ).astype(BF16)
    rc = lax.broadcasted_iota(jnp.int32, (rows, width), 0) // group
    own = (rc % fuse) == lax.broadcasted_iota(jnp.int32, (rows, width), 1) // body

    def spread(r, _):
        wt = w_ref[r, :body, :].astype(F32).T.astype(BF16)
        wide[r] = jnp.where(own, mm(wt, turn), 0.0).astype(BF16)
        return _

    lax.fori_loop(0, n, spread, 0, unroll=4)
    fetch.wait()
    for load in loads:
        load.wait()
    par = par_ref[0]

    def one(r):
        outs = []
        for g in range(combos // fuse):
            tiles = []
            for c in range(fuse):
                for i in range(share):
                    tiles.append(v_ref[idx_s[g * fuse + c, r * share + i]])
            at = slice(g * fuse * group, (g + 1) * fuse * group)
            outs.append(mm(wide[r, at, :], jnp.concatenate(tiles, axis=0)))
        return jnp.concatenate(outs, axis=0)

    def step(m, _):
        send_ref[m] = one(2 * m + 1 - par).astype(BF16)
        keep_ref[m] = one(2 * m + par)
        return _

    lax.fori_loop(0, n // 2, step, 0, unroll=2)


def holder(par, w, v, share, combos):
    n, wire, rows = w.shape
    vmem = pl.BlockSpec(memory_space=pltpu.VMEM)
    body = BLOCK_TOKENS * share
    fuse = max(1, min(combos, 256 // body))
    return pl.pallas_call(
        functools.partial(holder_kernel, share, combos),
        out_shape=(
            jax.ShapeDtypeStruct((n // 2, rows, HEAD_SIZE), F32),
            jax.ShapeDtypeStruct((n // 2, rows, HEAD_SIZE), BF16),
        ),
        in_specs=[pl.BlockSpec(memory_space=pltpu.SMEM), vmem, pl.BlockSpec(memory_space=pl.ANY)],
        out_specs=(vmem, vmem),
        scratch_shapes=[
            pltpu.VMEM(v.shape, v.dtype),
            pltpu.VMEM((n, rows, fuse * body), BF16),
            pltpu.VMEM((combos, n * share), jnp.int32),
            pltpu.SMEM((combos, n * share), jnp.int32),
            pltpu.SemaphoreType.DMA((4,)),
            pltpu.SemaphoreType.DMA,
        ],
        compiler_params=pltpu.CompilerParams(vmem_limit_bytes=52 * 1024 * 1024),
        name="holder",
    )(par, w, v)


def per_device(
    queries, new_keys, incoming_values, key_left, right_key_factor, value_tile_store, slot_map, chosen, lengths,
):
    n = lax.axis_size("store")
    me = lax.axis_index("store")
    steps, _, heads, n_sel = chosen.shape
    blocks = slot_map.shape[2]
    combos = steps * heads
    share = max(1, blocks // n // 4)
    pool = value_tile_store.shape[0]
    w, fresh = owner(
        lengths, queries[:, 0], new_keys[:, 0], incoming_values[:, 0], key_left[0].T,
        right_key_factor[0], slot_map[0], chosen.reshape(combos, n_sel), share, n, pool,
    )
    w, store = lax.optimization_barrier((w, value_tile_store))
    tiles = store.reshape(pool, BLOCK_TOKENS, HEAD_SIZE)
    w = lax.all_to_all(w, "store", split_axis=0, concat_axis=0, tiled=True)
    par = (me % 2).astype(jnp.int32).reshape(1)
    keep, send = holder(par, w, tiles, share, combos)
    other = lax.ppermute(send, "store", [(i, i ^ 1) for i in range(n)])
    both = (keep + other.astype(F32)).astype(BF16)
    groups = [[i for i in range(n) if i % 2 == c] for c in range(2)]
    parts = lax.all_to_all(both, "store", split_axis=0, concat_axis=0, tiled=True, axis_index_groups=groups)
    out = fresh + jnp.sum(parts.astype(F32), axis=0)
    return out.astype(BF16).reshape(queries.shape)


def solution(mesh):
    in_specs = (
        P(None, ("groups", "store"), None),
        P(None, ("groups", "store"), None),
        P(None, ("groups", "store"), None),
        P(("groups", "store"), None, None),
        P(("groups", "store"), None, None),
        P(("groups", "store"), None),
        P(("groups", "store"), None, None),
        P(None, ("groups", "store"), None, None),
        P(("groups", "store")),
    )
    out_specs = P(None, ("groups", "store"), None)
    return jax.shard_map(
        per_device, mesh=mesh, in_specs=in_specs, out_specs=out_specs, check_vma=False
    )
```

```python
import functools

import jax
import jax.numpy as jnp
import numpy as np
from jax import lax
from jax.experimental import pallas as pl
from jax.experimental.pallas import tpu as pltpu
from jax.sharding import PartitionSpec as P

HEAD_SIZE = 128
HALF = HEAD_SIZE // 2
BLOCK_TOKENS = 8
LANES = 128
ROPE_BASE = 500000.0
NT = (((1,), (1,)), ((), ()))
NN = (((1,), (0,)), ((), ()))
F32 = jnp.float32
BF16 = jnp.bfloat16


def mm(a, b, dims=NN):
    return lax.dot_general(a, b, dims, preferred_element_type=F32)


def rope_tables(blocks):
    exponent = -(np.arange(HALF, dtype=np.float32) * np.float32(2.0) / np.float32(HEAD_SIZE))
    freq = np.float32(ROPE_BASE) ** exponent
    pos = np.arange(blocks * BLOCK_TOKENS).reshape(-1, LANES, BLOCK_TOKENS).transpose(0, 2, 1)
    pos = pos.reshape(-1, 2 * LANES).astype(np.float32)
    angle = (pos[:, None, :] * freq[None, :, None]).astype(np.float64)
    keys = np.stack([np.cos(angle), np.sin(angle)], axis=1).astype(np.float32)
    freq = np.concatenate([freq, freq]).astype(np.float64)
    rows = np.arange(-(-(blocks + 2) // 8) * 8, dtype=np.float64)[:, None] * BLOCK_TOKENS
    offs = np.arange(BLOCK_TOKENS, dtype=np.float64)[:, None]
    base = np.stack([np.cos(rows * freq), np.sin(rows * freq)]).astype(np.float32)
    off = np.stack([np.cos(offs * freq), np.sin(offs * freq)]).astype(np.float32)
    return keys, base, off


def split3(x):
    a = x.astype(BF16)
    r = x - a.astype(F32)
    b = r.astype(BF16)
    return a, b, (r - b.astype(F32)).astype(BF16)


def owner_kernel(
    share, pool, keepers, len_ref, q_hbm, nk_hbm, iv_hbm, kl_hbm, rk_hbm, sm_hbm, ch_hbm, tab_hbm, base_hbm, off_hbm,
    w_ref, fresh_ref,
    q_ref, nk_ref, iv_ref, kl_ref, rk_ref, sm_ref, ch_ref, tab_ref, base_ref, off_ref, sems,
    lp, kk, rt, qp, qr, nr, vr, sc, fs_scr, fm_scr, fw_scr, pm, got_scr, lhs_scr, osc,
):
    rank, tokens = kl_ref.shape
    heads, blocks = sm_ref.shape
    combos, n_sel = ch_ref.shape
    steps = combos // heads
    rows = qr.shape[0]
    group = rows // combos
    planes = osc.shape[0]
    slots = osc.shape[2]
    pairs = heads // 2
    per_step = heads * group
    chunks = blocks // LANES
    scale = HEAD_SIZE ** -0.5
    length = len_ref[0]

    half = 4 * LANES
    count = [0]

    def bring(src, dst):
        move = pltpu.make_async_copy(src, dst, sems.at[count[0]])
        move.start()
        count[0] += 1
        return move

    lefts = []
    for t in range(chunks):
        at = slice(t * 2 * half, (t + 1) * 2 * half)
        lefts.append(bring(kl_hbm.at[:, at], kl_ref.at[:, at]))
    right = bring(rk_hbm, rk_ref)
    small = [bring(*x) for x in (
        (q_hbm, q_ref), (nk_hbm, nk_ref), (iv_hbm, iv_ref), (sm_hbm, sm_ref), (ch_hbm, ch_ref),
        (base_hbm, base_ref), (off_hbm, off_ref),
    )]
    per_chunk = BLOCK_TOKENS // 2
    tables = []
    for t in range(chunks):
        at = slice(t * per_chunk, (t + 1) * per_chunk)
        tables.append(bring(tab_hbm.at[at], tab_ref.at[at]))

    lane = lax.broadcasted_iota(jnp.int32, (1, HEAD_SIZE), 1)
    low = lane < HALF
    to = lax.broadcasted_iota(jnp.int32, (1, half), 1)
    pm[...] = jnp.where(
        lax.broadcasted_iota(jnp.int32, (half, half), 0) == (to % HALF) * BLOCK_TOKENS + to // HALF, 1.0, 0.0
    ).astype(BF16)

    for i in range(chunks):
        lefts[i].wait()
        at = i * 2 * half
        a = mm(kl_ref[:, at:at + half], pm[...])
        b = mm(kl_ref[:, at + half:at + 2 * half], pm[...])
        for m in range(BLOCK_TOKENS // 2):
            x = a[:, m * LANES:(m + 1) * LANES]
            y = b[:, m * LANES:(m + 1) * LANES]
            even = jnp.where(low, x, pltpu.roll(y, HALF, 1))
            odd = jnp.where(low, pltpu.roll(x, HALF, 1), y)
            lp[i * per_chunk + m] = jnp.concatenate([even, odd], axis=1).astype(BF16)

    right.wait()
    for h in range(heads):
        rt[h * HEAD_SIZE:(h + 1) * HEAD_SIZE, :] = (
            rk_ref[:, h * HEAD_SIZE:(h + 1) * HEAD_SIZE].astype(F32).T.astype(BF16)
        )

    for move in small:
        move.wait()
    x = q_ref[...].astype(F32)
    for k in range(per_step):
        qr[pl.ds(k, steps, stride=per_step), :] = x[:, k * HEAD_SIZE:(k + 1) * HEAD_SIZE]
    x = nk_ref[...].astype(F32)
    y = iv_ref[...].astype(F32)
    for k in range(heads):
        nr[pl.ds(k, steps, stride=heads), :] = x[:, k * HEAD_SIZE:(k + 1) * HEAD_SIZE]
        vr[pl.ds(k, steps, stride=heads), :] = y[:, k * HEAD_SIZE:(k + 1) * HEAD_SIZE]

    sign = jnp.where(low, -1.0, 1.0).astype(F32)

    def angle(position):
        b = position // BLOCK_TOKENS
        j = position - b * BLOCK_TOKENS
        cb = base_ref[0, pl.ds(b, 1), :]
        sb = base_ref[1, pl.ds(b, 1), :]
        cj = off_ref[0, pl.ds(j, 1), :]
        sj = off_ref[1, pl.ds(j, 1), :]
        return cb * cj - sb * sj, (sb * cj + cb * sj) * sign

    fresh_keys = []
    for s in range(steps):
        c, sn = angle(length + s)
        x = qr[s * per_step:(s + 1) * per_step, :]
        x = x * c + pltpu.roll(x, HALF, 1) * sn
        qr[s * per_step:(s + 1) * per_step, :] = x.astype(BF16).astype(F32)
        y = nr[s * heads:(s + 1) * heads, :]
        fresh_keys.append(y * c + pltpu.roll(y, HALF, 1) * sn)
    fk = jnp.concatenate(fresh_keys, axis=0).astype(BF16)
    fs = mm(qr[...].astype(BF16), fk, NT) * scale
    ri = lax.broadcasted_iota(jnp.int32, fs.shape, 0)
    ci = lax.broadcasted_iota(jnp.int32, fs.shape, 1)
    keep = jnp.logical_and((ri // group) % heads == ci % heads, ci // heads <= ri // per_step)
    fs = jnp.where(keep, fs, -jnp.inf)
    fs_scr[...] = fs
    fm_scr[...] = jnp.max(fs, axis=1, keepdims=True)

    for p in range(pairs):
        pieces = []
        for s in range(steps):
            for hh in range(2):
                start = s * per_step + (2 * p + hh) * group
                x = qr[start:start + group, :]
                z = jnp.zeros_like(x)
                pieces.append(jnp.concatenate([x, z] if hh == 0 else [z, x], axis=1))
        qp[p] = jnp.concatenate(pieces, axis=0).astype(BF16)

    def keys(i):
        ct = tab_ref[i, 0]
        st = tab_ref[i, 1]
        raw = mm(rt[...], lp[i])
        for h in range(heads):
            a = raw[h * HEAD_SIZE:h * HEAD_SIZE + HALF, :]
            c = raw[h * HEAD_SIZE + HALF:(h + 1) * HEAD_SIZE, :]
            kk[i, h * HEAD_SIZE:(h + 1) * HEAD_SIZE, :] = jnp.concatenate(
                [a * ct - c * st, c * ct + a * st], axis=0
            ).astype(BF16)

    for t in range(chunks):
        tables[t].wait()
        for i in range(t * per_chunk, (t + 1) * per_chunk):
            keys(i)

    def scores(i):
        at = i // per_chunk
        j = 2 * (i % per_chunk)
        for p in range(pairs):
            out = mm(qp[p], kk[i, 2 * p * HEAD_SIZE:2 * (p + 1) * HEAD_SIZE, :]) * scale
            for s in range(steps):
                to_rows = slice(s * per_step + 2 * p * group, s * per_step + 2 * (p + 1) * group)
                for jj in range(2):
                    sc[at, j + jj, to_rows, :] = out[s * 2 * group:(s + 1) * 2 * group, jj * LANES:(jj + 1) * LANES]

    for i in range(lp.shape[0]):
        scores(i)

    wide = steps * n_sel
    entry = lax.broadcasted_iota(jnp.int32, (1, wide), 1)
    block_i = lax.broadcasted_iota(jnp.int32, (blocks, wide), 0)
    keeper_i = lax.broadcasted_iota(jnp.int32, (keepers, wide), 0)
    slot_i = lax.broadcasted_iota(jnp.int32, (wide, steps * slots), 1).astype(F32)
    e0 = lax.broadcasted_iota(jnp.int32, (wide, wide), 0)
    e1 = lax.broadcasted_iota(jnp.int32, (wide, wide), 1)
    before = jnp.where(jnp.logical_and(e0 // n_sel == e1 // n_sel, e0 < e1), 1.0, 0.0).astype(BF16)
    sub = lax.broadcasted_iota(jnp.int32, (16, blocks), 0)
    sub_e = lax.broadcasted_iota(jnp.int32, (8, wide), 0)

    size = BLOCK_TOKENS * group
    heres = [
        [slice((s * heads + h) * group, (s * heads + h + 1) * group) for s in range(steps)] for h in range(heads)
    ]
    chosen = [
        jnp.concatenate([ch_ref[s * heads + h:s * heads + h + 1, :] for s in range(steps)], axis=1)
        for h in range(heads)
    ]
    for h in range(heads):
        hot = jnp.where(block_i == chosen[h], 1.0, 0.0).astype(BF16)
        row = sm_ref[h:h + 1, :]
        kb = row // pool
        inside = row - kb * pool
        hi = inside // 256
        lo = inside - hi * 256
        extra = jnp.where(sub == 0, hi, jnp.where(sub == 1, lo, jnp.where(sub == 2, kb, 0))).astype(F32).astype(BF16)
        terms = [extra]
        for s in range(steps):
            x = jnp.concatenate(
                [
                    jnp.concatenate([sc[t, j, heres[h][s], :] for t in range(chunks)], axis=1)
                    for j in range(BLOCK_TOKENS)
                ],
                axis=0,
            )
            terms += split3(x)
        got_scr[h] = mm(jnp.concatenate(terms, axis=0), hot)

    kbs = [got_scr[h, 2:3, :] for h in range(heads)]
    khs = jnp.concatenate([jnp.where(keeper_i == kb.astype(jnp.int32), 1.0, 0.0) for kb in kbs], axis=0)
    ranks = khs * mm(khs.astype(BF16), before)
    first = ((entry // n_sel) * slots).astype(F32)
    slot = jnp.concatenate(
        [
            kbs[h] * share + first + jnp.sum(ranks[h * keepers:(h + 1) * keepers], axis=0, keepdims=True)
            for h in range(heads)
        ],
        axis=0,
    ).T

    for h in range(heads):
        xs = None
        for s in range(steps):
            at = 16 + 3 * s * size
            g = (got_scr[h, at:at + size] + got_scr[h, at + size:at + 2 * size]) + got_scr[h, at + 2 * size:at + 3 * size]
            xs = g if xs is None else jnp.where(entry // n_sel == s, g, xs)
        pos = chosen[h] * BLOCK_TOKENS
        xs = [
            jnp.where(pos + j < length, xs[j * group:(j + 1) * group, :], -jnp.inf) for j in range(BLOCK_TOKENS)
        ]
        most = functools.reduce(jnp.maximum, xs)
        tops = []
        top = None
        for s in range(steps):
            mine = entry // n_sel == s
            t = jnp.max(jnp.where(mine, most, -jnp.inf), axis=1, keepdims=True)
            t = jnp.maximum(t, fm_scr[heres[h][s], :])
            tops.append(t)
            top = jnp.broadcast_to(t, most.shape) if top is None else jnp.where(mine, t, top)
        es = [jnp.exp(x - top) for x in xs]
        added = functools.reduce(jnp.add, es)
        inv = None
        for s in range(steps):
            mine = entry // n_sel == s
            fe = jnp.exp(fs_scr[heres[h][s], :] - tops[s])
            total = jnp.sum(jnp.where(mine, added, 0.0), axis=1, keepdims=True)
            one = 1.0 / (total + jnp.sum(fe, axis=1, keepdims=True))
            fw_scr[heres[h][s], :] = fe * one
            inv = jnp.broadcast_to(one, most.shape) if inv is None else jnp.where(mine, one, inv)
        tail = jnp.where(sub_e < 2, got_scr[h, :8, :], 0.0)
        lhs_scr[h] = jnp.concatenate([e * inv for e in es] + [tail, jnp.zeros_like(tail)], axis=0).astype(BF16)

    for h in range(heads):
        pick = jnp.where(slot_i == slot[:, h:h + 1], 1.0, 0.0).astype(BF16)
        o = mm(lhs_scr[h], pick)
        for t in range(planes):
            for s in range(steps):
                osc[t, heres[h][s], :] = o[t * group:(t + 1) * group, s * slots:(s + 1) * slots]

    fresh_ref[...] = mm(fw_scr[...].astype(BF16), vr[...].astype(BF16))

    turned = [osc[t].T for t in range(planes)]
    if share % 8 == 0:
        for k in range(keepers):
            w_ref[k] = jnp.concatenate([t[k * share:(k + 1) * share, :] for t in turned], axis=0).astype(BF16)
    else:
        for t in range(planes):
            w_ref[t] = turned[t].astype(BF16)


def owner(length, q, nk, iv, kl, rk, sm, ch, share, n, pool):
    rank, tokens = kl.shape
    heads, blocks = sm.shape
    combos, n_sel = ch.shape
    rows = q.size // HEAD_SIZE
    fresh_rows = nk.size // HEAD_SIZE
    slots = n * share
    planes = BLOCK_TOKENS + 1
    pairs = heads // 2
    direct = share % 8 == 0
    w_shape = (n, planes * share, rows) if direct else (planes, slots, rows)
    hbm = pl.BlockSpec(memory_space=pl.ANY)
    vmem = pl.BlockSpec(memory_space=pltpu.VMEM)
    operands = (q, nk, iv, kl, rk, sm, ch) + tuple(jnp.asarray(t) for t in rope_tables(blocks))
    w, fresh = pl.pallas_call(
        functools.partial(owner_kernel, share, pool, n),
        out_shape=(jax.ShapeDtypeStruct(w_shape, BF16), jax.ShapeDtypeStruct((rows, HEAD_SIZE), F32)),
        in_specs=[pl.BlockSpec(memory_space=pltpu.SMEM)] + [hbm] * len(operands),
        out_specs=(vmem, vmem),
        scratch_shapes=[pltpu.VMEM(x.shape, x.dtype) for x in operands] + [
            pltpu.SemaphoreType.DMA((len(operands) - 2 + 2 * (blocks // LANES),)),
            pltpu.VMEM((tokens // (2 * LANES), rank, 2 * LANES), BF16),
            pltpu.VMEM((tokens // (2 * LANES), heads * HEAD_SIZE, 2 * LANES), BF16),
            pltpu.VMEM((heads * HEAD_SIZE, rank), BF16),
            pltpu.VMEM((pairs, rows // pairs, 2 * HEAD_SIZE), BF16),
            pltpu.VMEM((rows, HEAD_SIZE), F32),
            pltpu.VMEM((fresh_rows, HEAD_SIZE), F32),
            pltpu.VMEM((fresh_rows, HEAD_SIZE), F32),
            pltpu.VMEM((blocks // LANES, BLOCK_TOKENS, rows, LANES), F32),
            pltpu.VMEM((rows, fresh_rows), F32),
            pltpu.VMEM((rows, 1), F32),
            pltpu.VMEM((rows, fresh_rows), F32),
            pltpu.VMEM((4 * LANES, 4 * LANES), BF16),
            pltpu.VMEM((heads, 16 + 3 * rows // heads * BLOCK_TOKENS, combos // heads * n_sel), F32),
            pltpu.VMEM((heads, (planes + 1) * rows // combos, combos // heads * n_sel), BF16),
            pltpu.VMEM((planes, rows, slots), F32),
        ],
        compiler_params=pltpu.CompilerParams(vmem_limit_bytes=60 * 1024 * 1024),
        name="owner",
    )(length, *operands)
    if not direct:
        w = w.reshape(planes, n, share, rows).transpose(1, 0, 2, 3).reshape(n, planes * share, rows)
    return w, fresh


def tile_kernel(v_hbm, out_hbm, buf, out, sems, out_sems):
    pool, width = buf.shape
    chunks = width // LANES
    parts = sems.shape[0]
    size = pool // parts
    run = 32
    loads = []
    for i in range(parts):
        at = pl.ds(i * size, size)
        load = pltpu.make_async_copy(v_hbm.at[at, :], buf.at[at, :], sems.at[i])
        load.start()
        loads.append(load)
    n = run * chunks
    to = lax.broadcasted_iota(jnp.int32, (n, n), 0)
    turn = jnp.where(
        lax.broadcasted_iota(jnp.int32, (n, n), 1) == (to % chunks) * run + to // chunks, 1.0, 0.0
    ).astype(BF16)

    def one(k, _):
        at = pl.multiple_of(k * 2 * run, 2 * run)
        x = jnp.concatenate([
            jnp.concatenate(
                [buf[pl.ds(at + g * run, run), c * LANES:(c + 1) * LANES] for c in range(chunks)], axis=0
            ) for g in range(2)
        ], axis=1)
        y = mm(turn, x)
        for g in range(2):
            out[pl.ds(at + g * run, run), :, :] = (
                y[:, g * LANES:(g + 1) * LANES].reshape(run, chunks, LANES).astype(BF16)
            )
        return _

    per = size // (2 * run)
    stores = []
    for i in range(parts):
        loads[i].wait()
        lax.fori_loop(i * per, (i + 1) * per, one, 0, unroll=16)
        at = pl.ds(i * size, size)
        store = pltpu.make_async_copy(out.at[at], out_hbm.at[at], out_sems.at[i])
        store.start()
        stores.append(store)
    for store in stores:
        store.wait()


def tile_rows(v):
    pool, width = v.shape
    shape = (pool, width // LANES, LANES)
    return pl.pallas_call(
        tile_kernel,
        out_shape=jax.ShapeDtypeStruct(shape, v.dtype),
        in_specs=[pl.BlockSpec(memory_space=pl.ANY)],
        out_specs=pl.BlockSpec(memory_space=pl.ANY),
        scratch_shapes=[
            pltpu.VMEM(v.shape, v.dtype),
            pltpu.VMEM(shape, v.dtype),
            pltpu.SemaphoreType.DMA((4,)),
            pltpu.SemaphoreType.DMA((4,)),
        ],
        compiler_params=pltpu.CompilerParams(vmem_limit_bytes=54 * 1024 * 1024),
        cost_estimate=pl.CostEstimate(flops=2 * pool * width * 256, bytes_accessed=4 * pool * width, transcendentals=0),
        name="tile_rows",
    )(v)


def holder_kernel(share, combos, par_ref, w_ref, v_hbm, keep_ref, send_ref, v_ref, wide, idx_v, idx_s, vsems, isem):
    n, wire, rows = w_ref.shape
    group = rows // combos
    body = BLOCK_TOKENS * share
    fuse = max(1, min(combos, 256 // body))
    parts = vsems.shape[0]
    size = v_ref.shape[0] // parts
    loads = []
    for i in range(parts):
        at = pl.ds(i * size, size)
        load = pltpu.make_async_copy(v_hbm.at[at], v_ref.at[at], vsems.at[i])
        load.start()
        loads.append(load)
    raw = w_ref[:, body:body + share, :].astype(F32).reshape(n * share, rows).astype(BF16)
    ci = lax.broadcasted_iota(jnp.int32, (combos, rows), 0)
    li = lax.broadcasted_iota(jnp.int32, (combos, rows), 1)
    sel = jnp.where(li == ci * group, 256.0, jnp.where(li == ci * group + 1, 1.0, 0.0)).astype(BF16)
    idx_v[...] = mm(sel, raw, NT).astype(jnp.int32)
    fetch = pltpu.make_async_copy(idx_v, idx_s, isem)
    fetch.start()
    width = fuse * body
    a = lax.broadcasted_iota(jnp.int32, (body, width), 0)
    b = lax.broadcasted_iota(jnp.int32, (body, width), 1) % body
    turn = jnp.where(
        jnp.logical_and(a // share == b % BLOCK_TOKENS, a % share == b // BLOCK_TOKENS), 1.0, 0.0
    ).astype(BF16)
    rc = lax.broadcasted_iota(jnp.int32, (rows, width), 0) // group
    own = (rc % fuse) == lax.broadcasted_iota(jnp.int32, (rows, width), 1) // body

    def spread(r, _):
        wt = w_ref[r, :body, :].astype(F32).T.astype(BF16)
        wide[r] = jnp.where(own, mm(wt, turn), 0.0).astype(BF16)
        return _

    lax.fori_loop(0, n, spread, 0, unroll=4)
    fetch.wait()
    for load in loads:
        load.wait()
    par = par_ref[0]

    def one(r):
        outs = []
        for g in range(combos // fuse):
            tiles = []
            for c in range(fuse):
                for i in range(share):
                    tiles.append(v_ref[idx_s[g * fuse + c, r * share + i]])
            at = slice(g * fuse * group, (g + 1) * fuse * group)
            outs.append(mm(wide[r, at, :], jnp.concatenate(tiles, axis=0)))
        return jnp.concatenate(outs, axis=0)

    def step(m, _):
        send_ref[m] = one(2 * m + 1 - par).astype(BF16)
        keep_ref[m] = one(2 * m + par)
        return _

    lax.fori_loop(0, n // 2, step, 0, unroll=2)


def holder(par, w, v, share, combos):
    n, wire, rows = w.shape
    vmem = pl.BlockSpec(memory_space=pltpu.VMEM)
    body = BLOCK_TOKENS * share
    fuse = max(1, min(combos, 256 // body))
    return pl.pallas_call(
        functools.partial(holder_kernel, share, combos),
        out_shape=(
            jax.ShapeDtypeStruct((n // 2, rows, HEAD_SIZE), F32),
            jax.ShapeDtypeStruct((n // 2, rows, HEAD_SIZE), BF16),
        ),
        in_specs=[pl.BlockSpec(memory_space=pltpu.SMEM), vmem, pl.BlockSpec(memory_space=pl.ANY)],
        out_specs=(vmem, vmem),
        scratch_shapes=[
            pltpu.VMEM(v.shape, v.dtype),
            pltpu.VMEM((n, rows, fuse * body), BF16),
            pltpu.VMEM((combos, n * share), jnp.int32),
            pltpu.SMEM((combos, n * share), jnp.int32),
            pltpu.SemaphoreType.DMA((4,)),
            pltpu.SemaphoreType.DMA,
        ],
        compiler_params=pltpu.CompilerParams(vmem_limit_bytes=52 * 1024 * 1024),
        name="holder",
    )(par, w, v)


def per_device(
    queries, new_keys, incoming_values, key_left, right_key_factor, value_tile_store, slot_map, chosen, lengths,
):
    n = lax.axis_size("store")
    me = lax.axis_index("store")
    steps, _, heads, n_sel = chosen.shape
    blocks = slot_map.shape[2]
    combos = steps * heads
    share = max(1, blocks // n // 4)
    pool = value_tile_store.shape[0]
    w, fresh = owner(
        lengths, queries[:, 0], new_keys[:, 0], incoming_values[:, 0], key_left[0].T,
        right_key_factor[0], slot_map[0], chosen.reshape(combos, n_sel), share, n, pool,
    )
    w, store = lax.optimization_barrier((w, value_tile_store))
    tiles = tile_rows(store)
    w = lax.all_to_all(w, "store", split_axis=0, concat_axis=0, tiled=True)
    par = (me % 2).astype(jnp.int32).reshape(1)
    keep, send = holder(par, w, tiles, share, combos)
    other = lax.ppermute(send, "store", [(i, i ^ 1) for i in range(n)])
    both = (keep + other.astype(F32)).astype(BF16)
    groups = [[i for i in range(n) if i % 2 == c] for c in range(2)]
    parts = lax.all_to_all(both, "store", split_axis=0, concat_axis=0, tiled=True, axis_index_groups=groups)
    out = fresh + jnp.sum(parts.astype(F32), axis=0)
    return out.astype(BF16).reshape(queries.shape)


def solution(mesh):
    in_specs = (
        P(None, ("groups", "store"), None),
        P(None, ("groups", "store"), None),
        P(None, ("groups", "store"), None),
        P(("groups", "store"), None, None),
        P(("groups", "store"), None, None),
        P(("groups", "store"), None),
        P(("groups", "store"), None, None),
        P(None, ("groups", "store"), None, None),
        P(("groups", "store")),
    )
    out_specs = P(None, ("groups", "store"), None)
    return jax.shard_map(
        per_device, mesh=mesh, in_specs=in_specs, out_specs=out_specs, check_vma=False
    )
```

```python
import functools

import jax
import jax.numpy as jnp
import numpy as np
from jax import lax
from jax.experimental import pallas as pl
from jax.experimental.pallas import tpu as pltpu
from jax.sharding import PartitionSpec as P

HEAD_SIZE = 128
HALF = HEAD_SIZE // 2
BLOCK_TOKENS = 8
LANES = 128
FAR = 64
ROPE_BASE = 500000.0
NT = (((1,), (1,)), ((), ()))
NN = (((1,), (0,)), ((), ()))
F32 = jnp.float32
BF16 = jnp.bfloat16


def mm(a, b, dims=NN):
    return lax.dot_general(a, b, dims, preferred_element_type=F32)


def rope_tables(blocks):
    exponent = -(np.arange(HALF, dtype=np.float32) * np.float32(2.0) / np.float32(HEAD_SIZE))
    freq = np.float32(ROPE_BASE) ** exponent
    pos = np.arange(blocks * BLOCK_TOKENS).reshape(-1, LANES, BLOCK_TOKENS).transpose(0, 2, 1)
    pos = pos.reshape(-1, 2 * LANES).astype(np.float32)
    angle = (pos[:, None, :] * freq[None, :, None]).astype(np.float64)
    keys = np.stack([np.cos(angle), np.sin(angle)], axis=1).astype(np.float32)
    freq = np.concatenate([freq, freq]).astype(np.float64)
    far = np.arange(-(-(blocks * BLOCK_TOKENS // FAR + 2) // 8) * 8, dtype=np.float64) * FAR
    angle = np.concatenate([far, np.arange(FAR, dtype=np.float64)])[:, None] * freq
    return keys, np.stack([np.cos(angle), np.sin(angle)]).astype(np.float32)


def split3(x):
    a = x.astype(BF16)
    r = x - a.astype(F32)
    b = r.astype(BF16)
    return a, b, (r - b.astype(F32)).astype(BF16)


def owner_kernel(
    share, pool, keepers, len_ref, q_hbm, nk_hbm, iv_hbm, kl_hbm, rk_hbm, sm_hbm, ch_hbm, tab_hbm, turn_hbm,
    w_ref, fresh_ref,
    q_ref, nk_ref, iv_ref, kl_ref, rk_ref, sm_ref, ch_ref, tab_ref, turn_ref, sems,
    lp, kk, rt, qp, qr, nr, vr, sc, fs_scr, fm_scr, fw_scr, pm, got_scr, lhs_scr, osc,
):
    rank, tokens = kl_ref.shape
    heads, blocks = sm_ref.shape
    combos, n_sel = ch_ref.shape
    steps = combos // heads
    rows = qr.shape[0]
    group = rows // combos
    planes = osc.shape[0]
    slots = osc.shape[2]
    pairs = heads // 2
    per_step = heads * group
    chunks = blocks // LANES
    scale = HEAD_SIZE ** -0.5
    length = len_ref[0]

    half = 4 * LANES
    count = [0]

    def bring(src, dst):
        move = pltpu.make_async_copy(src, dst, sems.at[count[0]])
        move.start()
        count[0] += 1
        return move

    small = [bring(*x) for x in ((q_hbm, q_ref), (nk_hbm, nk_ref), (iv_hbm, iv_ref), (turn_hbm, turn_ref))]
    right = bring(rk_hbm, rk_ref)
    left = bring(kl_hbm, kl_ref)
    table = bring(tab_hbm, tab_ref)
    maps = [bring(sm_hbm, sm_ref), bring(ch_hbm, ch_ref)]
    per_chunk = BLOCK_TOKENS // 2

    lane = lax.broadcasted_iota(jnp.int32, (1, HEAD_SIZE), 1)
    low = lane < HALF
    to = lax.broadcasted_iota(jnp.int32, (1, half), 1)
    pm[...] = jnp.where(
        lax.broadcasted_iota(jnp.int32, (half, half), 0) == (to % HALF) * BLOCK_TOKENS + to // HALF, 1.0, 0.0
    ).astype(BF16)

    for move in small:
        move.wait()
    x = q_ref[...].astype(F32)
    for k in range(per_step):
        qr[pl.ds(k, steps, stride=per_step), :] = x[:, k * HEAD_SIZE:(k + 1) * HEAD_SIZE]
    x = nk_ref[...].astype(F32)
    y = iv_ref[...].astype(F32)
    for k in range(heads):
        nr[pl.ds(k, steps, stride=heads), :] = x[:, k * HEAD_SIZE:(k + 1) * HEAD_SIZE]
        vr[pl.ds(k, steps, stride=heads), :] = y[:, k * HEAD_SIZE:(k + 1) * HEAD_SIZE]

    sign = jnp.where(low, -1.0, 1.0).astype(F32)

    def angle(position):
        b = position // FAR
        j = position - b * FAR + turn_ref.shape[1] - FAR
        cb = turn_ref[0, pl.ds(b, 1), :]
        sb = turn_ref[1, pl.ds(b, 1), :]
        cj = turn_ref[0, pl.ds(j, 1), :]
        sj = turn_ref[1, pl.ds(j, 1), :]
        return cb * cj - sb * sj, (sb * cj + cb * sj) * sign

    fresh_keys = []
    for s in range(steps):
        c, sn = angle(length + s)
        x = qr[s * per_step:(s + 1) * per_step, :]
        x = x * c + pltpu.roll(x, HALF, 1) * sn
        qr[s * per_step:(s + 1) * per_step, :] = x.astype(BF16).astype(F32)
        y = nr[s * heads:(s + 1) * heads, :]
        fresh_keys.append(y * c + pltpu.roll(y, HALF, 1) * sn)
    fk = jnp.concatenate(fresh_keys, axis=0).astype(BF16)
    fs = mm(qr[...].astype(BF16), fk, NT) * scale
    ri = lax.broadcasted_iota(jnp.int32, fs.shape, 0)
    ci = lax.broadcasted_iota(jnp.int32, fs.shape, 1)
    keep = jnp.logical_and((ri // group) % heads == ci % heads, ci // heads <= ri // per_step)
    fs = jnp.where(keep, fs, -jnp.inf)
    fs_scr[...] = fs
    fm_scr[...] = jnp.max(fs, axis=1, keepdims=True)

    for p in range(pairs):
        pieces = []
        for s in range(steps):
            for hh in range(2):
                start = s * per_step + (2 * p + hh) * group
                x = qr[start:start + group, :]
                z = jnp.zeros_like(x)
                pieces.append(jnp.concatenate([x, z] if hh == 0 else [z, x], axis=1))
        qp[p] = jnp.concatenate(pieces, axis=0).astype(BF16)

    right.wait()
    for h in range(heads):
        rt[h * HEAD_SIZE:(h + 1) * HEAD_SIZE, :] = (
            rk_ref[:, h * HEAD_SIZE:(h + 1) * HEAD_SIZE].astype(F32).T.astype(BF16)
        )

    left.wait()

    for i in range(chunks):
        at = i * 2 * half
        a = mm(kl_ref[:, at:at + half], pm[...])
        b = mm(kl_ref[:, at + half:at + 2 * half], pm[...])
        for m in range(BLOCK_TOKENS // 2):
            x = a[:, m * LANES:(m + 1) * LANES]
            y = b[:, m * LANES:(m + 1) * LANES]
            even = jnp.where(low, x, pltpu.roll(y, HALF, 1))
            odd = jnp.where(low, pltpu.roll(x, HALF, 1), y)
            lp[i * per_chunk + m] = jnp.concatenate([even, odd], axis=1).astype(BF16)

    def keys(i):
        ct = tab_ref[i, 0]
        st = tab_ref[i, 1]
        raw = mm(rt[...], lp[i])
        for h in range(heads):
            a = raw[h * HEAD_SIZE:h * HEAD_SIZE + HALF, :]
            c = raw[h * HEAD_SIZE + HALF:(h + 1) * HEAD_SIZE, :]
            kk[i, h * HEAD_SIZE:(h + 1) * HEAD_SIZE, :] = jnp.concatenate(
                [a * ct - c * st, c * ct + a * st], axis=0
            ).astype(BF16)

    def scores(i):
        at = i // per_chunk
        j = 2 * (i % per_chunk)
        for p in range(pairs):
            out = mm(qp[p], kk[i, 2 * p * HEAD_SIZE:2 * (p + 1) * HEAD_SIZE, :]) * scale
            for s in range(steps):
                to_rows = slice(s * per_step + 2 * p * group, s * per_step + 2 * (p + 1) * group)
                for jj in range(2):
                    sc[at, j + jj, to_rows, :] = out[s * 2 * group:(s + 1) * 2 * group, jj * LANES:(jj + 1) * LANES]

    table.wait()
    for i in range(lp.shape[0]):
        keys(i)
        if i > 0:
            scores(i - 1)
    scores(lp.shape[0] - 1)

    for move in maps:
        move.wait()
    wide = steps * n_sel
    entry = lax.broadcasted_iota(jnp.int32, (1, wide), 1)
    block_i = lax.broadcasted_iota(jnp.int32, (blocks, wide), 0)
    keeper_i = lax.broadcasted_iota(jnp.int32, (keepers, wide), 0)
    slot_i = lax.broadcasted_iota(jnp.int32, (wide, steps * slots), 1).astype(F32)
    e0 = lax.broadcasted_iota(jnp.int32, (wide, wide), 0)
    e1 = lax.broadcasted_iota(jnp.int32, (wide, wide), 1)
    before = jnp.where(jnp.logical_and(e0 // n_sel == e1 // n_sel, e0 < e1), 1.0, 0.0).astype(BF16)
    sub = lax.broadcasted_iota(jnp.int32, (16, blocks), 0)
    sub_e = lax.broadcasted_iota(jnp.int32, (8, wide), 0)

    size = BLOCK_TOKENS * group
    heres = [
        [slice((s * heads + h) * group, (s * heads + h + 1) * group) for s in range(steps)] for h in range(heads)
    ]
    chosen = [
        jnp.concatenate([ch_ref[s * heads + h:s * heads + h + 1, :] for s in range(steps)], axis=1)
        for h in range(heads)
    ]
    for h in range(heads):
        hot = jnp.where(block_i == chosen[h], 1.0, 0.0).astype(BF16)
        row = sm_ref[h:h + 1, :]
        kb = row // pool
        inside = row - kb * pool
        hi = inside // 256
        lo = inside - hi * 256
        extra = jnp.where(sub == 0, hi, jnp.where(sub == 1, lo, jnp.where(sub == 2, kb, 0))).astype(F32).astype(BF16)
        terms = [extra]
        for s in range(steps):
            x = jnp.concatenate(
                [
                    jnp.concatenate([sc[t, j, heres[h][s], :] for t in range(chunks)], axis=1)
                    for j in range(BLOCK_TOKENS)
                ],
                axis=0,
            )
            terms += split3(x)
        got_scr[h] = mm(jnp.concatenate(terms, axis=0), hot)

    kbs = [got_scr[h, 2:3, :] for h in range(heads)]
    khs = jnp.concatenate([jnp.where(keeper_i == kb.astype(jnp.int32), 1.0, 0.0) for kb in kbs], axis=0)
    ranks = khs * mm(khs.astype(BF16), before)
    first = ((entry // n_sel) * slots).astype(F32)
    slot = jnp.concatenate(
        [
            kbs[h] * share + first + jnp.sum(ranks[h * keepers:(h + 1) * keepers], axis=0, keepdims=True)
            for h in range(heads)
        ],
        axis=0,
    ).T

    for h in range(heads):
        xs = None
        for s in range(steps):
            at = 16 + 3 * s * size
            g = (got_scr[h, at:at + size] + got_scr[h, at + size:at + 2 * size]) + got_scr[h, at + 2 * size:at + 3 * size]
            xs = g if xs is None else jnp.where(entry // n_sel == s, g, xs)
        pos = chosen[h] * BLOCK_TOKENS
        xs = [
            jnp.where(pos + j < length, xs[j * group:(j + 1) * group, :], -jnp.inf) for j in range(BLOCK_TOKENS)
        ]
        most = functools.reduce(jnp.maximum, xs)
        tops = []
        top = None
        for s in range(steps):
            mine = entry // n_sel == s
            t = jnp.max(jnp.where(mine, most, -jnp.inf), axis=1, keepdims=True)
            t = jnp.maximum(t, fm_scr[heres[h][s], :])
            tops.append(t)
            top = jnp.broadcast_to(t, most.shape) if top is None else jnp.where(mine, t, top)
        es = [jnp.exp(x - top) for x in xs]
        added = functools.reduce(jnp.add, es)
        inv = None
        for s in range(steps):
            mine = entry // n_sel == s
            fe = jnp.exp(fs_scr[heres[h][s], :] - tops[s])
            total = jnp.sum(jnp.where(mine, added, 0.0), axis=1, keepdims=True)
            one = 1.0 / (total + jnp.sum(fe, axis=1, keepdims=True))
            fw_scr[heres[h][s], :] = fe * one
            inv = jnp.broadcast_to(one, most.shape) if inv is None else jnp.where(mine, one, inv)
        tail = jnp.where(sub_e < 2, got_scr[h, :8, :], 0.0)
        lhs_scr[h] = jnp.concatenate([e * inv for e in es] + [tail, jnp.zeros_like(tail)], axis=0).astype(BF16)

    for h in range(heads):
        pick = jnp.where(slot_i == slot[:, h:h + 1], 1.0, 0.0).astype(BF16)
        o = mm(lhs_scr[h], pick)
        for t in range(planes):
            for s in range(steps):
                osc[t, heres[h][s], :] = o[t * group:(t + 1) * group, s * slots:(s + 1) * slots]

    fresh_ref[...] = mm(fw_scr[...].astype(BF16), vr[...].astype(BF16))

    turned = [osc[t].T for t in range(planes)]
    if share % 8 == 0:
        for k in range(keepers):
            w_ref[k] = jnp.concatenate([t[k * share:(k + 1) * share, :] for t in turned], axis=0).astype(BF16)
    else:
        for t in range(planes):
            w_ref[t] = turned[t].astype(BF16)


def owner(length, q, nk, iv, kl, rk, sm, ch, share, n, pool):
    rank, tokens = kl.shape
    heads, blocks = sm.shape
    combos, n_sel = ch.shape
    rows = q.size // HEAD_SIZE
    fresh_rows = nk.size // HEAD_SIZE
    slots = n * share
    planes = BLOCK_TOKENS + 1
    pairs = heads // 2
    direct = share % 8 == 0
    w_shape = (n, planes * share, rows) if direct else (planes, slots, rows)
    hbm = pl.BlockSpec(memory_space=pl.ANY)
    vmem = pl.BlockSpec(memory_space=pltpu.VMEM)
    operands = (q, nk, iv, kl, rk, sm, ch) + tuple(jnp.asarray(t) for t in rope_tables(blocks))
    w, fresh = pl.pallas_call(
        functools.partial(owner_kernel, share, pool, n),
        out_shape=(jax.ShapeDtypeStruct(w_shape, BF16), jax.ShapeDtypeStruct((rows, HEAD_SIZE), F32)),
        in_specs=[pl.BlockSpec(memory_space=pltpu.SMEM)] + [hbm] * len(operands),
        out_specs=(vmem, vmem),
        scratch_shapes=[pltpu.VMEM(x.shape, x.dtype) for x in operands] + [
            pltpu.SemaphoreType.DMA((len(operands),)),
            pltpu.VMEM((tokens // (2 * LANES), rank, 2 * LANES), BF16),
            pltpu.VMEM((tokens // (2 * LANES), heads * HEAD_SIZE, 2 * LANES), BF16),
            pltpu.VMEM((heads * HEAD_SIZE, rank), BF16),
            pltpu.VMEM((pairs, rows // pairs, 2 * HEAD_SIZE), BF16),
            pltpu.VMEM((rows, HEAD_SIZE), F32),
            pltpu.VMEM((fresh_rows, HEAD_SIZE), F32),
            pltpu.VMEM((fresh_rows, HEAD_SIZE), F32),
            pltpu.VMEM((blocks // LANES, BLOCK_TOKENS, rows, LANES), F32),
            pltpu.VMEM((rows, fresh_rows), F32),
            pltpu.VMEM((rows, 1), F32),
            pltpu.VMEM((rows, fresh_rows), F32),
            pltpu.VMEM((4 * LANES, 4 * LANES), BF16),
            pltpu.VMEM((heads, 16 + 3 * rows // heads * BLOCK_TOKENS, combos // heads * n_sel), F32),
            pltpu.VMEM((heads, (planes + 1) * rows // combos, combos // heads * n_sel), BF16),
            pltpu.VMEM((planes, rows, slots), F32),
        ],
        compiler_params=pltpu.CompilerParams(vmem_limit_bytes=60 * 1024 * 1024),
        name="owner",
    )(length, *operands)
    if not direct:
        w = w.reshape(planes, n, share, rows).transpose(1, 0, 2, 3).reshape(n, planes * share, rows)
    return w, fresh


def tile_kernel(v_hbm, out_hbm, buf, out, sems, out_sems):
    pool, width = buf.shape
    chunks = width // LANES
    parts = sems.shape[0]
    size = pool // parts
    run = 32
    loads = []
    for i in range(parts):
        at = pl.ds(i * size, size)
        load = pltpu.make_async_copy(v_hbm.at[at, :], buf.at[at, :], sems.at[i])
        load.start()
        loads.append(load)
    n = run * chunks
    to = lax.broadcasted_iota(jnp.int32, (n, n), 0)
    turn = jnp.where(
        lax.broadcasted_iota(jnp.int32, (n, n), 1) == (to % chunks) * run + to // chunks, 1.0, 0.0
    ).astype(BF16)

    def one(k, _):
        at = pl.multiple_of(k * 2 * run, 2 * run)
        x = jnp.concatenate([
            jnp.concatenate(
                [buf[pl.ds(at + g * run, run), c * LANES:(c + 1) * LANES] for c in range(chunks)], axis=0
            ) for g in range(2)
        ], axis=1)
        y = mm(turn, x)
        for g in range(2):
            out[pl.ds(at + g * run, run), :, :] = (
                y[:, g * LANES:(g + 1) * LANES].reshape(run, chunks, LANES).astype(BF16)
            )
        return _

    per = size // (2 * run)
    stores = []
    for i in range(parts):
        loads[i].wait()
        lax.fori_loop(i * per, (i + 1) * per, one, 0, unroll=16)
        at = pl.ds(i * size, size)
        store = pltpu.make_async_copy(out.at[at], out_hbm.at[at], out_sems.at[i])
        store.start()
        stores.append(store)
    for store in stores:
        store.wait()


def tile_rows(v):
    pool, width = v.shape
    shape = (pool, width // LANES, LANES)
    return pl.pallas_call(
        tile_kernel,
        out_shape=jax.ShapeDtypeStruct(shape, v.dtype),
        in_specs=[pl.BlockSpec(memory_space=pl.ANY)],
        out_specs=pl.BlockSpec(memory_space=pl.ANY),
        scratch_shapes=[
            pltpu.VMEM(v.shape, v.dtype),
            pltpu.VMEM(shape, v.dtype),
            pltpu.SemaphoreType.DMA((4,)),
            pltpu.SemaphoreType.DMA((4,)),
        ],
        compiler_params=pltpu.CompilerParams(vmem_limit_bytes=54 * 1024 * 1024),
        cost_estimate=pl.CostEstimate(flops=2 * pool * width * 256, bytes_accessed=4 * pool * width, transcendentals=0),
        name="tile_rows",
    )(v)


def holder_kernel(share, combos, par_ref, w_ref, v_hbm, keep_ref, send_ref, v_ref, wide, idx_v, idx_s, vsems, isem):
    n, wire, rows = w_ref.shape
    group = rows // combos
    body = BLOCK_TOKENS * share
    fuse = max(1, min(combos, 256 // body))
    parts = vsems.shape[0]
    size = v_ref.shape[0] // parts
    loads = []
    for i in range(parts):
        at = pl.ds(i * size, size)
        load = pltpu.make_async_copy(v_hbm.at[at], v_ref.at[at], vsems.at[i])
        load.start()
        loads.append(load)
    raw = w_ref[:, body:body + share, :].astype(F32).reshape(n * share, rows).astype(BF16)
    ci = lax.broadcasted_iota(jnp.int32, (combos, rows), 0)
    li = lax.broadcasted_iota(jnp.int32, (combos, rows), 1)
    sel = jnp.where(li == ci * group, 256.0, jnp.where(li == ci * group + 1, 1.0, 0.0)).astype(BF16)
    idx_v[...] = mm(sel, raw, NT).astype(jnp.int32)
    fetch = pltpu.make_async_copy(idx_v, idx_s, isem)
    fetch.start()
    width = fuse * body
    a = lax.broadcasted_iota(jnp.int32, (body, width), 0)
    b = lax.broadcasted_iota(jnp.int32, (body, width), 1) % body
    turn = jnp.where(
        jnp.logical_and(a // share == b % BLOCK_TOKENS, a % share == b // BLOCK_TOKENS), 1.0, 0.0
    ).astype(BF16)
    rc = lax.broadcasted_iota(jnp.int32, (rows, width), 0) // group
    own = (rc % fuse) == lax.broadcasted_iota(jnp.int32, (rows, width), 1) // body

    def spread(r, _):
        wt = w_ref[r, :body, :].astype(F32).T.astype(BF16)
        wide[r] = jnp.where(own, mm(wt, turn), 0.0).astype(BF16)
        return _

    lax.fori_loop(0, n, spread, 0, unroll=4)
    fetch.wait()
    for load in loads:
        load.wait()
    par = par_ref[0]

    def one(r):
        outs = []
        for g in range(combos // fuse):
            tiles = []
            for c in range(fuse):
                for i in range(share):
                    tiles.append(v_ref[idx_s[g * fuse + c, r * share + i]])
            at = slice(g * fuse * group, (g + 1) * fuse * group)
            outs.append(mm(wide[r, at, :], jnp.concatenate(tiles, axis=0)))
        return jnp.concatenate(outs, axis=0)

    def step(m, _):
        send_ref[m] = one(2 * m + 1 - par).astype(BF16)
        keep_ref[m] = one(2 * m + par)
        return _

    lax.fori_loop(0, n // 2, step, 0, unroll=min(8, n // 2))


def holder(par, w, v, share, combos):
    n, wire, rows = w.shape
    vmem = pl.BlockSpec(memory_space=pltpu.VMEM)
    body = BLOCK_TOKENS * share
    fuse = max(1, min(combos, 256 // body))
    return pl.pallas_call(
        functools.partial(holder_kernel, share, combos),
        out_shape=(
            jax.ShapeDtypeStruct((n // 2, rows, HEAD_SIZE), F32),
            jax.ShapeDtypeStruct((n // 2, rows, HEAD_SIZE), BF16),
        ),
        in_specs=[pl.BlockSpec(memory_space=pltpu.SMEM), vmem, pl.BlockSpec(memory_space=pl.ANY)],
        out_specs=(vmem, vmem),
        scratch_shapes=[
            pltpu.VMEM(v.shape, v.dtype),
            pltpu.VMEM((n, rows, fuse * body), BF16),
            pltpu.VMEM((combos, n * share), jnp.int32),
            pltpu.SMEM((combos, n * share), jnp.int32),
            pltpu.SemaphoreType.DMA((4,)),
            pltpu.SemaphoreType.DMA,
        ],
        compiler_params=pltpu.CompilerParams(vmem_limit_bytes=52 * 1024 * 1024),
        name="holder",
    )(par, w, v)


def per_device(
    queries, new_keys, incoming_values, key_left, right_key_factor, value_tile_store, slot_map, chosen, lengths,
):
    n = lax.axis_size("store")
    me = lax.axis_index("store")
    steps, _, heads, n_sel = chosen.shape
    blocks = slot_map.shape[2]
    combos = steps * heads
    share = max(1, blocks // n // 4)
    pool = value_tile_store.shape[0]
    w, fresh = owner(
        lengths, queries[:, 0], new_keys[:, 0], incoming_values[:, 0], key_left[0].T,
        right_key_factor[0], slot_map[0], chosen.reshape(combos, n_sel), share, n, pool,
    )
    w, store = lax.optimization_barrier((w, value_tile_store))
    tiles = tile_rows(store)
    w = lax.all_to_all(w, "store", split_axis=0, concat_axis=0, tiled=True)
    par = (me % 2).astype(jnp.int32).reshape(1)
    keep, send = holder(par, w, tiles, share, combos)
    other = lax.ppermute(send, "store", [(i, i ^ 1) for i in range(n)])
    both = (keep + other.astype(F32)).astype(BF16)
    groups = [[i for i in range(n) if i % 2 == c] for c in range(2)]
    parts = lax.all_to_all(both, "store", split_axis=0, concat_axis=0, tiled=True, axis_index_groups=groups)
    out = fresh + jnp.sum(parts.astype(F32), axis=0)
    return out.astype(BF16).reshape(queries.shape)


def solution(mesh):
    in_specs = (
        P(None, ("groups", "store"), None),
        P(None, ("groups", "store"), None),
        P(None, ("groups", "store"), None),
        P(("groups", "store"), None, None),
        P(("groups", "store"), None, None),
        P(("groups", "store"), None),
        P(("groups", "store"), None, None),
        P(None, ("groups", "store"), None, None),
        P(("groups", "store")),
    )
    out_specs = P(None, ("groups", "store"), None)
    return jax.shard_map(
        per_device, mesh=mesh, in_specs=in_specs, out_specs=out_specs, check_vma=False
    )
```

```python
import functools

import jax
import jax.numpy as jnp
import numpy as np
from jax import lax
from jax.experimental import pallas as pl
from jax.experimental.pallas import tpu as pltpu
from jax.sharding import PartitionSpec as P

HEAD_SIZE = 128
HALF = HEAD_SIZE // 2
BLOCK_TOKENS = 8
LANES = 128
FAR = 64
ROPE_BASE = 500000.0
NT = (((1,), (1,)), ((), ()))
NN = (((1,), (0,)), ((), ()))
F32 = jnp.float32
BF16 = jnp.bfloat16


def mm(a, b, dims=NN):
    return lax.dot_general(a, b, dims, preferred_element_type=F32)


def rope_tables(blocks):
    exponent = -(np.arange(HALF, dtype=np.float32) * np.float32(2.0) / np.float32(HEAD_SIZE))
    freq = np.float32(ROPE_BASE) ** exponent
    pos = np.arange(blocks * BLOCK_TOKENS).reshape(-1, LANES, BLOCK_TOKENS).transpose(0, 2, 1)
    pos = pos.reshape(-1, 2 * LANES).astype(np.float32)
    angle = (pos[:, None, :] * freq[None, :, None]).astype(np.float64)
    keys = np.stack([np.cos(angle), np.sin(angle)], axis=1).astype(np.float32)
    freq = np.concatenate([freq, freq]).astype(np.float64)
    far = np.arange(-(-(blocks * BLOCK_TOKENS // FAR + 2) // 8) * 8, dtype=np.float64) * FAR
    angle = np.concatenate([far, np.arange(FAR, dtype=np.float64)])[:, None] * freq
    return keys, np.stack([np.cos(angle), np.sin(angle)]).astype(np.float32)


def split3(x):
    a = x.astype(BF16)
    r = x - a.astype(F32)
    b = r.astype(BF16)
    return a, b, (r - b.astype(F32)).astype(BF16)


def owner_kernel(
    share, pool, keepers, len_ref, q_hbm, nk_hbm, iv_hbm, kl_hbm, rk_hbm, sm_hbm, ch_hbm, tab_hbm, turn_hbm,
    w_hbm, fresh_ref,
    q_ref, nk_ref, iv_ref, kl_ref, rk_ref, sm_ref, ch_ref, tab_ref, turn_ref, sems,
    lp, kk, rt, qp, qr, nr, vr, sc, fs_scr, fm_scr, fw_scr, pm, got_scr, lhs_scr, osc, w_ref, w_sems,
):
    rank, tokens = kl_ref.shape
    heads, blocks = sm_ref.shape
    combos, n_sel = ch_ref.shape
    steps = combos // heads
    rows = qr.shape[0]
    group = rows // combos
    planes = osc.shape[0]
    slots = osc.shape[2]
    pairs = heads // 2
    per_step = heads * group
    chunks = blocks // LANES
    scale = HEAD_SIZE ** -0.5
    length = len_ref[0]

    half = 4 * LANES
    count = [0]

    def bring(src, dst):
        move = pltpu.make_async_copy(src, dst, sems.at[count[0]])
        move.start()
        count[0] += 1
        return move

    small = [bring(*x) for x in ((q_hbm, q_ref), (nk_hbm, nk_ref), (iv_hbm, iv_ref), (turn_hbm, turn_ref))]
    right = bring(rk_hbm, rk_ref)
    left = bring(kl_hbm, kl_ref)
    table = bring(tab_hbm, tab_ref)
    maps = [bring(sm_hbm, sm_ref), bring(ch_hbm, ch_ref)]
    per_chunk = BLOCK_TOKENS // 2

    lane = lax.broadcasted_iota(jnp.int32, (1, HEAD_SIZE), 1)
    low = lane < HALF
    to = lax.broadcasted_iota(jnp.int32, (1, half), 1)
    pm[...] = jnp.where(
        lax.broadcasted_iota(jnp.int32, (half, half), 0) == (to % HALF) * BLOCK_TOKENS + to // HALF, 1.0, 0.0
    ).astype(BF16)

    for move in small:
        move.wait()
    x = q_ref[...].astype(F32)
    for k in range(per_step):
        qr[pl.ds(k, steps, stride=per_step), :] = x[:, k * HEAD_SIZE:(k + 1) * HEAD_SIZE]
    x = nk_ref[...].astype(F32)
    y = iv_ref[...].astype(F32)
    for k in range(heads):
        nr[pl.ds(k, steps, stride=heads), :] = x[:, k * HEAD_SIZE:(k + 1) * HEAD_SIZE]
        vr[pl.ds(k, steps, stride=heads), :] = y[:, k * HEAD_SIZE:(k + 1) * HEAD_SIZE]

    sign = jnp.where(low, -1.0, 1.0).astype(F32)

    def angle(position):
        b = position // FAR
        j = position - b * FAR + turn_ref.shape[1] - FAR
        cb = turn_ref[0, pl.ds(b, 1), :]
        sb = turn_ref[1, pl.ds(b, 1), :]
        cj = turn_ref[0, pl.ds(j, 1), :]
        sj = turn_ref[1, pl.ds(j, 1), :]
        return cb * cj - sb * sj, (sb * cj + cb * sj) * sign

    fresh_keys = []
    for s in range(steps):
        c, sn = angle(length + s)
        x = qr[s * per_step:(s + 1) * per_step, :]
        x = x * c + pltpu.roll(x, HALF, 1) * sn
        qr[s * per_step:(s + 1) * per_step, :] = x.astype(BF16).astype(F32)
        y = nr[s * heads:(s + 1) * heads, :]
        fresh_keys.append(y * c + pltpu.roll(y, HALF, 1) * sn)
    fk = jnp.concatenate(fresh_keys, axis=0).astype(BF16)
    fs = mm(qr[...].astype(BF16), fk, NT) * scale
    ri = lax.broadcasted_iota(jnp.int32, fs.shape, 0)
    ci = lax.broadcasted_iota(jnp.int32, fs.shape, 1)
    keep = jnp.logical_and((ri // group) % heads == ci % heads, ci // heads <= ri // per_step)
    fs = jnp.where(keep, fs, -jnp.inf)
    fs_scr[...] = fs
    fm_scr[...] = jnp.max(fs, axis=1, keepdims=True)

    for p in range(pairs):
        pieces = []
        for s in range(steps):
            for hh in range(2):
                start = s * per_step + (2 * p + hh) * group
                x = qr[start:start + group, :]
                z = jnp.zeros_like(x)
                pieces.append(jnp.concatenate([x, z] if hh == 0 else [z, x], axis=1))
        qp[p] = jnp.concatenate(pieces, axis=0).astype(BF16)

    right.wait()
    for h in range(heads):
        rt[h * HEAD_SIZE:(h + 1) * HEAD_SIZE, :] = (
            rk_ref[:, h * HEAD_SIZE:(h + 1) * HEAD_SIZE].astype(F32).T.astype(BF16)
        )

    left.wait()

    for i in range(chunks):
        at = i * 2 * half
        a = mm(kl_ref[:, at:at + half], pm[...])
        b = mm(kl_ref[:, at + half:at + 2 * half], pm[...])
        for m in range(BLOCK_TOKENS // 2):
            x = a[:, m * LANES:(m + 1) * LANES]
            y = b[:, m * LANES:(m + 1) * LANES]
            even = jnp.where(low, x, pltpu.roll(y, HALF, 1))
            odd = jnp.where(low, pltpu.roll(x, HALF, 1), y)
            lp[i * per_chunk + m] = jnp.concatenate([even, odd], axis=1).astype(BF16)

    def keys(i):
        ct = tab_ref[i, 0]
        st = tab_ref[i, 1]
        raw = mm(rt[...], lp[i])
        for h in range(heads):
            a = raw[h * HEAD_SIZE:h * HEAD_SIZE + HALF, :]
            c = raw[h * HEAD_SIZE + HALF:(h + 1) * HEAD_SIZE, :]
            kk[i, h * HEAD_SIZE:(h + 1) * HEAD_SIZE, :] = jnp.concatenate(
                [a * ct - c * st, c * ct + a * st], axis=0
            ).astype(BF16)

    def scores(i):
        at = i // per_chunk
        j = 2 * (i % per_chunk)
        for p in range(pairs):
            out = mm(qp[p], kk[i, 2 * p * HEAD_SIZE:2 * (p + 1) * HEAD_SIZE, :]) * scale
            for s in range(steps):
                to_rows = slice(s * per_step + 2 * p * group, s * per_step + 2 * (p + 1) * group)
                for jj in range(2):
                    sc[at, j + jj, to_rows, :] = out[s * 2 * group:(s + 1) * 2 * group, jj * LANES:(jj + 1) * LANES]

    table.wait()
    for i in range(lp.shape[0]):
        keys(i)
        if i > 0:
            scores(i - 1)
    scores(lp.shape[0] - 1)

    for move in maps:
        move.wait()
    wide = steps * n_sel
    entry = lax.broadcasted_iota(jnp.int32, (1, wide), 1)
    block_i = lax.broadcasted_iota(jnp.int32, (blocks, wide), 0)
    keeper_i = lax.broadcasted_iota(jnp.int32, (keepers, wide), 0)
    slot_i = lax.broadcasted_iota(jnp.int32, (wide, steps * slots), 1).astype(F32)
    e0 = lax.broadcasted_iota(jnp.int32, (wide, wide), 0)
    e1 = lax.broadcasted_iota(jnp.int32, (wide, wide), 1)
    before = jnp.where(jnp.logical_and(e0 // n_sel == e1 // n_sel, e0 < e1), 1.0, 0.0).astype(BF16)
    sub = lax.broadcasted_iota(jnp.int32, (16, blocks), 0)
    sub_e = lax.broadcasted_iota(jnp.int32, (8, wide), 0)

    size = BLOCK_TOKENS * group
    heres = [
        [slice((s * heads + h) * group, (s * heads + h + 1) * group) for s in range(steps)] for h in range(heads)
    ]
    chosen = [
        jnp.concatenate([ch_ref[s * heads + h:s * heads + h + 1, :] for s in range(steps)], axis=1)
        for h in range(heads)
    ]
    for h in range(heads):
        hot = jnp.where(block_i == chosen[h], 1.0, 0.0).astype(BF16)
        row = sm_ref[h:h + 1, :]
        kb = row // pool
        inside = row - kb * pool
        hi = inside // 256
        lo = inside - hi * 256
        extra = jnp.where(sub == 0, hi, jnp.where(sub == 1, lo, jnp.where(sub == 2, kb, 0))).astype(F32).astype(BF16)
        terms = [extra]
        for s in range(steps):
            x = jnp.concatenate(
                [
                    jnp.concatenate([sc[t, j, heres[h][s], :] for t in range(chunks)], axis=1)
                    for j in range(BLOCK_TOKENS)
                ],
                axis=0,
            )
            terms += split3(x)
        got_scr[h] = mm(jnp.concatenate(terms, axis=0), hot)

    kbs = [got_scr[h, 2:3, :] for h in range(heads)]
    khs = jnp.concatenate([jnp.where(keeper_i == kb.astype(jnp.int32), 1.0, 0.0) for kb in kbs], axis=0)
    ranks = khs * mm(khs.astype(BF16), before)
    first = ((entry // n_sel) * slots).astype(F32)
    slot = jnp.concatenate(
        [
            kbs[h] * share + first + jnp.sum(ranks[h * keepers:(h + 1) * keepers], axis=0, keepdims=True)
            for h in range(heads)
        ],
        axis=0,
    ).T

    for h in range(heads):
        xs = None
        for s in range(steps):
            at = 16 + 3 * s * size
            g = (got_scr[h, at:at + size] + got_scr[h, at + size:at + 2 * size]) + got_scr[h, at + 2 * size:at + 3 * size]
            xs = g if xs is None else jnp.where(entry // n_sel == s, g, xs)
        pos = chosen[h] * BLOCK_TOKENS
        xs = [
            jnp.where(pos + j < length, xs[j * group:(j + 1) * group, :], -jnp.inf) for j in range(BLOCK_TOKENS)
        ]
        most = functools.reduce(jnp.maximum, xs)
        tops = []
        top = None
        for s in range(steps):
            mine = entry // n_sel == s
            t = jnp.max(jnp.where(mine, most, -jnp.inf), axis=1, keepdims=True)
            t = jnp.maximum(t, fm_scr[heres[h][s], :])
            tops.append(t)
            top = jnp.broadcast_to(t, most.shape) if top is None else jnp.where(mine, t, top)
        es = [jnp.exp(x - top) for x in xs]
        added = functools.reduce(jnp.add, es)
        inv = None
        for s in range(steps):
            mine = entry // n_sel == s
            fe = jnp.exp(fs_scr[heres[h][s], :] - tops[s])
            total = jnp.sum(jnp.where(mine, added, 0.0), axis=1, keepdims=True)
            one = 1.0 / (total + jnp.sum(fe, axis=1, keepdims=True))
            fw_scr[heres[h][s], :] = fe * one
            inv = jnp.broadcast_to(one, most.shape) if inv is None else jnp.where(mine, one, inv)
        tail = jnp.where(sub_e < 2, got_scr[h, :8, :], 0.0)
        lhs_scr[h] = jnp.concatenate([e * inv for e in es] + [tail, jnp.zeros_like(tail)], axis=0).astype(BF16)

    for h in range(heads):
        pick = jnp.where(slot_i == slot[:, h:h + 1], 1.0, 0.0).astype(BF16)
        o = mm(lhs_scr[h], pick)
        for t in range(planes):
            for s in range(steps):
                osc[t, heres[h][s], :] = o[t * group:(t + 1) * group, s * slots:(s + 1) * slots]

    fresh_ref[...] = mm(fw_scr[...].astype(BF16), vr[...].astype(BF16))

    turned = [osc[t].T for t in range(planes)]
    size = w_ref.shape[0] // w_sems.shape[0]
    sends = []
    for k in range(w_ref.shape[0]):
        if share % 8 == 0:
            w_ref[k] = jnp.concatenate([t[k * share:(k + 1) * share, :] for t in turned], axis=0).astype(BF16)
        else:
            w_ref[k] = turned[k].astype(BF16)
        if (k + 1) % size == 0:
            at = pl.ds(k + 1 - size, size)
            send = pltpu.make_async_copy(w_ref.at[at], w_hbm.at[at], w_sems.at[k // size])
            send.start()
            sends.append(send)
    for send in sends:
        send.wait()


def owner(length, q, nk, iv, kl, rk, sm, ch, share, n, pool):
    rank, tokens = kl.shape
    heads, blocks = sm.shape
    combos, n_sel = ch.shape
    rows = q.size // HEAD_SIZE
    fresh_rows = nk.size // HEAD_SIZE
    slots = n * share
    planes = BLOCK_TOKENS + 1
    pairs = heads // 2
    direct = share % 8 == 0
    w_shape = (n, planes * share, rows) if direct else (planes, slots, rows)
    hbm = pl.BlockSpec(memory_space=pl.ANY)
    vmem = pl.BlockSpec(memory_space=pltpu.VMEM)
    operands = (q, nk, iv, kl, rk, sm, ch) + tuple(jnp.asarray(t) for t in rope_tables(blocks))
    w, fresh = pl.pallas_call(
        functools.partial(owner_kernel, share, pool, n),
        out_shape=(jax.ShapeDtypeStruct(w_shape, BF16), jax.ShapeDtypeStruct((rows, HEAD_SIZE), F32)),
        in_specs=[pl.BlockSpec(memory_space=pltpu.SMEM)] + [hbm] * len(operands),
        out_specs=(hbm, vmem),
        scratch_shapes=[pltpu.VMEM(x.shape, x.dtype) for x in operands] + [
            pltpu.SemaphoreType.DMA((len(operands),)),
            pltpu.VMEM((tokens // (2 * LANES), rank, 2 * LANES), BF16),
            pltpu.VMEM((tokens // (2 * LANES), heads * HEAD_SIZE, 2 * LANES), BF16),
            pltpu.VMEM((heads * HEAD_SIZE, rank), BF16),
            pltpu.VMEM((pairs, rows // pairs, 2 * HEAD_SIZE), BF16),
            pltpu.VMEM((rows, HEAD_SIZE), F32),
            pltpu.VMEM((fresh_rows, HEAD_SIZE), F32),
            pltpu.VMEM((fresh_rows, HEAD_SIZE), F32),
            pltpu.VMEM((blocks // LANES, BLOCK_TOKENS, rows, LANES), F32),
            pltpu.VMEM((rows, fresh_rows), F32),
            pltpu.VMEM((rows, 1), F32),
            pltpu.VMEM((rows, fresh_rows), F32),
            pltpu.VMEM((4 * LANES, 4 * LANES), BF16),
            pltpu.VMEM((heads, 16 + 3 * rows // heads * BLOCK_TOKENS, combos // heads * n_sel), F32),
            pltpu.VMEM((heads, (planes + 1) * rows // combos, combos // heads * n_sel), BF16),
            pltpu.VMEM((planes, rows, slots), F32),
            pltpu.VMEM(w_shape, BF16),
            pltpu.SemaphoreType.DMA((2 if direct else 1,)),
        ],
        compiler_params=pltpu.CompilerParams(vmem_limit_bytes=60 * 1024 * 1024),
        name="owner",
    )(length, *operands)
    if not direct:
        w = w.reshape(planes, n, share, rows).transpose(1, 0, 2, 3).reshape(n, planes * share, rows)
    return w, fresh


def tile_kernel(v_hbm, out_hbm, buf, out, sems, out_sems):
    pool, width = buf.shape
    chunks = width // LANES
    parts = sems.shape[0]
    size = pool // parts
    run = 32
    loads = []
    for i in range(parts):
        at = pl.ds(i * size, size)
        load = pltpu.make_async_copy(v_hbm.at[at, :], buf.at[at, :], sems.at[i])
        load.start()
        loads.append(load)
    n = run * chunks
    to = lax.broadcasted_iota(jnp.int32, (n, n), 0)
    turn = jnp.where(
        lax.broadcasted_iota(jnp.int32, (n, n), 1) == (to % chunks) * run + to // chunks, 1.0, 0.0
    ).astype(BF16)

    def one(k, _):
        at = pl.multiple_of(k * 2 * run, 2 * run)
        x = jnp.concatenate([
            jnp.concatenate(
                [buf[pl.ds(at + g * run, run), c * LANES:(c + 1) * LANES] for c in range(chunks)], axis=0
            ) for g in range(2)
        ], axis=1)
        y = mm(turn, x)
        for g in range(2):
            out[pl.ds(at + g * run, run), :, :] = (
                y[:, g * LANES:(g + 1) * LANES].reshape(run, chunks, LANES).astype(BF16)
            )
        return _

    per = size // (2 * run)
    stores = []
    for i in range(parts):
        loads[i].wait()
        lax.fori_loop(i * per, (i + 1) * per, one, 0, unroll=16)
        at = pl.ds(i * size, size)
        store = pltpu.make_async_copy(out.at[at], out_hbm.at[at], out_sems.at[i])
        store.start()
        stores.append(store)
    for store in stores:
        store.wait()


def tile_rows(v):
    pool, width = v.shape
    shape = (pool, width // LANES, LANES)
    return pl.pallas_call(
        tile_kernel,
        out_shape=jax.ShapeDtypeStruct(shape, v.dtype),
        in_specs=[pl.BlockSpec(memory_space=pl.ANY)],
        out_specs=pl.BlockSpec(memory_space=pl.ANY),
        scratch_shapes=[
            pltpu.VMEM(v.shape, v.dtype),
            pltpu.VMEM(shape, v.dtype),
            pltpu.SemaphoreType.DMA((4,)),
            pltpu.SemaphoreType.DMA((4,)),
        ],
        compiler_params=pltpu.CompilerParams(vmem_limit_bytes=54 * 1024 * 1024),
        cost_estimate=pl.CostEstimate(flops=2 * pool * width * 256, bytes_accessed=4 * pool * width, transcendentals=0),
        name="tile_rows",
    )(v)


def holder_kernel(share, combos, par_ref, w_ref, v_hbm, keep_ref, send_ref, v_ref, wide, idx_v, idx_s, vsems, isem):
    n, wire, rows = w_ref.shape
    group = rows // combos
    body = BLOCK_TOKENS * share
    fuse = max(1, min(combos, 256 // body))
    parts = vsems.shape[0]
    size = v_ref.shape[0] // parts
    loads = []
    for i in range(parts):
        at = pl.ds(i * size, size)
        load = pltpu.make_async_copy(v_hbm.at[at], v_ref.at[at], vsems.at[i])
        load.start()
        loads.append(load)
    raw = w_ref[:, body:body + share, :].astype(F32).reshape(n * share, rows).astype(BF16)
    ci = lax.broadcasted_iota(jnp.int32, (combos, rows), 0)
    li = lax.broadcasted_iota(jnp.int32, (combos, rows), 1)
    sel = jnp.where(li == ci * group, 256.0, jnp.where(li == ci * group + 1, 1.0, 0.0)).astype(BF16)
    idx_v[...] = mm(sel, raw, NT).astype(jnp.int32)
    fetch = pltpu.make_async_copy(idx_v, idx_s, isem)
    fetch.start()
    width = fuse * body
    a = lax.broadcasted_iota(jnp.int32, (body, width), 0)
    b = lax.broadcasted_iota(jnp.int32, (body, width), 1) % body
    turn = jnp.where(
        jnp.logical_and(a // share == b % BLOCK_TOKENS, a % share == b // BLOCK_TOKENS), 1.0, 0.0
    ).astype(BF16)
    rc = lax.broadcasted_iota(jnp.int32, (rows, width), 0) // group
    own = (rc % fuse) == lax.broadcasted_iota(jnp.int32, (rows, width), 1) // body

    def spread(r, _):
        wt = w_ref[r, :body, :].astype(F32).T.astype(BF16)
        wide[r] = jnp.where(own, mm(wt, turn), 0.0).astype(BF16)
        return _

    lax.fori_loop(0, n, spread, 0, unroll=4)
    fetch.wait()
    for load in loads:
        load.wait()
    par = par_ref[0]

    def one(r):
        outs = []
        for g in range(combos // fuse):
            tiles = []
            for c in range(fuse):
                for i in range(share):
                    tiles.append(v_ref[idx_s[g * fuse + c, r * share + i]])
            at = slice(g * fuse * group, (g + 1) * fuse * group)
            outs.append(mm(wide[r, at, :], jnp.concatenate(tiles, axis=0)))
        return jnp.concatenate(outs, axis=0)

    def step(m, _):
        send_ref[m] = one(2 * m + 1 - par).astype(BF16)
        keep_ref[m] = one(2 * m + par)
        return _

    lax.fori_loop(0, n // 2, step, 0, unroll=min(8, n // 2))


def holder(par, w, v, share, combos):
    n, wire, rows = w.shape
    vmem = pl.BlockSpec(memory_space=pltpu.VMEM)
    body = BLOCK_TOKENS * share
    fuse = max(1, min(combos, 256 // body))
    return pl.pallas_call(
        functools.partial(holder_kernel, share, combos),
        out_shape=(
            jax.ShapeDtypeStruct((n // 2, rows, HEAD_SIZE), F32),
            jax.ShapeDtypeStruct((n // 2, rows, HEAD_SIZE), BF16),
        ),
        in_specs=[pl.BlockSpec(memory_space=pltpu.SMEM), vmem, pl.BlockSpec(memory_space=pl.ANY)],
        out_specs=(vmem, vmem),
        scratch_shapes=[
            pltpu.VMEM(v.shape, v.dtype),
            pltpu.VMEM((n, rows, fuse * body), BF16),
            pltpu.VMEM((combos, n * share), jnp.int32),
            pltpu.SMEM((combos, n * share), jnp.int32),
            pltpu.SemaphoreType.DMA((4,)),
            pltpu.SemaphoreType.DMA,
        ],
        compiler_params=pltpu.CompilerParams(vmem_limit_bytes=52 * 1024 * 1024),
        name="holder",
    )(par, w, v)


def per_device(
    queries, new_keys, incoming_values, key_left, right_key_factor, value_tile_store, slot_map, chosen, lengths,
):
    n = lax.axis_size("store")
    me = lax.axis_index("store")
    steps, _, heads, n_sel = chosen.shape
    blocks = slot_map.shape[2]
    combos = steps * heads
    share = max(1, blocks // n // 4)
    pool = value_tile_store.shape[0]
    w, fresh = owner(
        lengths, queries[:, 0], new_keys[:, 0], incoming_values[:, 0], key_left[0].T,
        right_key_factor[0], slot_map[0], chosen.reshape(combos, n_sel), share, n, pool,
    )
    w, store = lax.optimization_barrier((w, value_tile_store))
    tiles = tile_rows(store)
    w = lax.all_to_all(w, "store", split_axis=0, concat_axis=0, tiled=True)
    par = (me % 2).astype(jnp.int32).reshape(1)
    keep, send = holder(par, w, tiles, share, combos)
    other = lax.ppermute(send, "store", [(i, i ^ 1) for i in range(n)])
    both = (keep + other.astype(F32)).astype(BF16)
    groups = [[i for i in range(n) if i % 2 == c] for c in range(2)]
    parts = lax.all_to_all(both, "store", split_axis=0, concat_axis=0, tiled=True, axis_index_groups=groups)
    out = fresh + jnp.sum(parts.astype(F32), axis=0)
    return out.astype(BF16).reshape(queries.shape)


def solution(mesh):
    in_specs = (
        P(None, ("groups", "store"), None),
        P(None, ("groups", "store"), None),
        P(None, ("groups", "store"), None),
        P(("groups", "store"), None, None),
        P(("groups", "store"), None, None),
        P(("groups", "store"), None),
        P(("groups", "store"), None, None),
        P(None, ("groups", "store"), None, None),
        P(("groups", "store")),
    )
    out_specs = P(None, ("groups", "store"), None)
    return jax.shard_map(
        per_device, mesh=mesh, in_specs=in_specs, out_specs=out_specs, check_vma=False
    )
```
